256 devices in a mesh: dp: 64 (over z, y, core), seq: 4 (over x).
Axes of the slice: x: 4, y: 4, z: 8, core: 2. Of those that a mesh axis runs over, the one named last changes fastest.
Arguments:
- loader_frames: bfloat16 [4, 4096, 640], P('seq', 'dp'), may hold values from -6 to 6
- block_dest: int32 [4, 4096], P('seq'), may hold values from 0 to 4095, as said below
- utt_lengths: int32 [64, 3], P('dp'), may hold values from 1 to 128, 256 in all within a row
- conv1_weight: bfloat16 [9, 512], replicated, may hold values from -2 to 2
- conv2_weight: bfloat16 [9, 512, 512], replicated, may hold values from -0.09375 to 0.09375
- proj_weight: bfloat16 [9728, 768], P('dp')
- gain_in: float32 [768], replicated, may hold values from 0.5 to 2
- point_in: bfloat16 [768, 1536], replicated, may hold values from -0.21875 to 0.21875
- taps: float32 [31, 768], replicated, may hold values from -1 to 1
- gain_mid: float32 [768], replicated, may hold values from 0.5 to 2
- point_out: bfloat16 [768, 768], replicated, may hold values from -0.21875 to 0.21875
- grad_encoded: bfloat16 [64, 512, 768], P('dp', 'seq'), may hold values from -6 to 6
Outputs:
- encoded: bfloat16 [64, 512, 768], P('dp', 'seq')
- grad_input: bfloat16 [64, 512, 768], P('dp', 'seq')
The draws below stay inside these ranges and needn't reach their ends.
Inputs may be any that keep to these rules, and one draw needn't show every extreme that they name: `block_dest`: for every seq index the row is a permutation. Of the 64 blocks at one dp index, at most 2 go to slots of one dp index (slot // 64), and every dp index sends exactly 2 to some dp index. `utt_lengths`: each row sums to 256; its longest utterance has exactly 128 blocks.
All inputs are finite; a program needn't handle non-finite values.
Results may differ from the reference program's by a relative error of at most 0.02.
Values may be sent and summed in bfloat16 or wider, within the bound.
No kernel may reach another device: no remote copies, remote signals or barrier semaphores. Data moves between devices by JAX's collectives and lax.ppermute only.
A program may use at most 128 MiB of HBM per device.

```python
import math
import jax
import jax.numpy as jnp
import numpy as np
from jax import lax

D = 768
C = 512
MEL = 80
KERNEL = 31
BLK = 8
UTTS = 3
BLK_DEV = 64
M2 = 19
STREAM = 512
N_DP = 64
N_SEQ = 4


def one_seat(seat_key):
    shift_key, dest_key, source_key, slot_key = jax.random.split(seat_key, 4)
    shifts = jax.random.permutation(shift_key, N_DP)
    dest_shuffle = jax.random.permutation(dest_key, N_DP)
    source_shuffle = jax.random.permutation(source_key, N_DP)
    shift_order = jnp.maximum(jnp.arange(BLK_DEV) - 1, 0) % N_DP
    dest_group = dest_shuffle[(source_shuffle[:, None] + shifts[shift_order][None, :]) % N_DP]
    slot_perms = jax.vmap(lambda one_key: jax.random.permutation(one_key, BLK_DEV))(jax.random.split(slot_key, N_DP))
    position = slot_perms[dest_group, jnp.arange(BLK_DEV)[None, :]]
    return (dest_group * BLK_DEV + position).reshape(-1).astype(jnp.int32)


def draw_block_dest(key, part):
    key = jax.random.fold_in(key, 5)
    seat_keys = jax.random.split(key, N_SEQ)
    return jax.vmap(one_seat)(seat_keys)


def draw_proj_weight(key, part):
    key = jax.random.fold_in(key, 11)
    row_count = M2 * C
    base_key = jax.random.fold_in(key, 0)
    values = jax.random.truncated_normal(base_key, -4.0, 4.0, (row_count, D), jnp.float32)
    return (values / math.sqrt(row_count)).astype(jnp.bfloat16)


def block_levels(rng, dims, cuts, smallest, top_value):
    level, own = 1.0, jax.random.fold_in(rng, 6)
    for axis_at, parts in cuts:
        heights = jnp.exp(jax.random.uniform(jax.random.fold_in(own, axis_at), (parts,), jnp.float32, smallest / len(cuts), top_value / len(cuts)))
        level = level * jnp.repeat(heights, dims[axis_at] // parts).reshape([-1 if axis == axis_at else 1 for axis in range(len(dims))])
    return level


def length_profile(amount, total, limit, lean):
    loads = [(1 << 20) // math.isqrt(standing ** lean) + 1 for standing in range(2, amount + 1)]
    surplus, holding = total - limit - (amount - 1), [1] * (amount - 1)
    while surplus > 0:
        movable = [i for i in range(amount - 1) if holding[i] < limit]
        mass, budget = sum([loads[i] for i in movable]), surplus
        for i in movable:
            extra = min(limit - holding[i], max(1, budget * loads[i] // mass), surplus)
            holding[i] = holding[i] + extra
            surplus = surplus - extra
    return np.array([limit] + holding)


def ragged_sizes(own_key, number_of, total, most, lean):
    if number_of == 2:
        one = jax.random.randint(own_key, (), max(1, total - most), min(most, total - 1) + 1)
        return jnp.stack([one, total - one])
    sizes = jnp.asarray(length_profile(number_of, total, most, lean), jnp.int32)
    pairs = (number_of - 1) // 2
    source_of, taker = sizes[1:1 + 2 * pairs:2], sizes[2:2 + 2 * pairs:2]
    margin = jnp.minimum(source_of - 1, most - taker)
    shifted = jax.random.randint(jax.random.fold_in(own_key, 1), (pairs,), 0, 1 << 20) % (margin + 1)
    sizes = sizes.at[1:1 + 2 * pairs:2].set(source_of - shifted).at[2:2 + 2 * pairs:2].set(taker + shifted)
    return sizes[jax.random.permutation(jax.random.fold_in(own_key, 2), number_of)]


def scatter_about(rng, dims, width, bound, cuts=(), kind=jnp.bfloat16):
    level = block_levels(rng, dims, cuts, -0.22, 0.18) if cuts else 1.0
    result = jax.random.normal(rng, dims, jnp.float32) * width * level
    return jnp.minimum(jnp.maximum(result, -bound), bound).astype(kind)


def setup_inputs(seed: int = 0) -> dict:
    keys = jax.random.split(jax.random.key(seed), 13)
    return {
        "loader_frames": scatter_about(keys[0], (N_SEQ, N_DP * BLK_DEV, BLK * MEL), 1.0, 6.0, ((0, 4), (1, 64))),
        "block_dest": draw_block_dest(jax.random.fold_in(keys[12], 71), 0),
        "utt_lengths": jax.vmap(lambda own: ragged_sizes(own, UTTS, N_SEQ * BLK_DEV, 2 * BLK_DEV, 2))(jax.random.split(keys[2], N_DP)).reshape((N_DP, UTTS)).astype(jnp.int32),
        "conv1_weight": scatter_about(keys[3], (9, C), 9 ** -0.5, 2.0),
        "conv2_weight": scatter_about(keys[4], (9, C, C), (9 * C) ** -0.5, 0.09375),
        "proj_weight": draw_proj_weight(jax.random.fold_in(keys[12], 71), 0),
        "gain_in": jnp.clip(jnp.exp(jax.random.uniform(keys[6], (D,), jnp.float32, math.log(0.5), math.log(2.0))), 0.5, 2.0),
        "point_in": scatter_about(keys[7], (D, 2 * D), D ** -0.5, 0.21875),
        "taps": scatter_about(keys[8], (KERNEL, D), KERNEL ** -0.5, 1.0, (), jnp.float32),
        "gain_mid": jnp.clip(jnp.exp(jax.random.uniform(keys[9], (D,), jnp.float32, math.log(0.5), math.log(2.0))), 0.5, 2.0),
        "point_out": scatter_about(keys[10], (D, D), D ** -0.5, 0.21875),
        "grad_encoded": scatter_about(keys[11], (N_DP, STREAM, D), 1.0, 6.0, ((0, 64), (1, 4))),
    }


def layer_norm(values):
    average = lax.optimization_barrier(jnp.mean(values, axis=-1, keepdims=True))
    centered = values - average
    inverse = lax.rsqrt(lax.optimization_barrier(jnp.mean(centered * centered, axis=-1, keepdims=True)) + 1e-05)
    return (centered * inverse, inverse)

def norm_back(d_normed, normed, inverse):
    return (d_normed - lax.optimization_barrier(jnp.mean(d_normed, axis=-1, keepdims=True)) - normed * lax.optimization_barrier(jnp.mean(d_normed * normed, axis=-1, keepdims=True))) * inverse

def swish_parts(values):
    logistic = jax.nn.sigmoid(values)
    return (values * logistic, logistic * (1.0 + values * (1.0 - logistic)))

def start_keep(is_start, per_block):
    frame_count = is_start.shape[0] * per_block
    leading = jnp.arange(frame_count) % per_block == 0
    return (1 - (jnp.repeat(is_start, per_block) & leading).astype(jnp.int32)).astype(jnp.bfloat16)

def first_conv(raw_ext, keep_left, conv1_weight):
    out_frames = (raw_ext.shape[0] - 1) // 2
    mel_bins = raw_ext.shape[1]
    out_bins = (mel_bins - 3) // 2 + 1
    patch_cols = []
    for row_tap in range(3):
        tap_rows = lax.slice(raw_ext, (row_tap, 0), (row_tap + 2 * out_frames - 1, mel_bins), (2, 1))
        if row_tap == 0:
            tap_rows = tap_rows * keep_left[:, None]
        for mel_tap in range(3):
            patch_cols.append(lax.slice(tap_rows, (0, mel_tap), (out_frames, mel_tap + 2 * out_bins - 1), (1, 2)))
    patches = jnp.stack(patch_cols, axis=-1).reshape(out_frames * out_bins, 9)
    response = jnp.dot(patches, conv1_weight, preferred_element_type=jnp.float32)
    return jnp.maximum(response, 0.0).astype(jnp.bfloat16).reshape(out_frames, out_bins, -1)

def second_conv(conv_ext, keep_left, conv2_weight):
    out_frames = (conv_ext.shape[0] - 1) // 2
    in_bins = conv_ext.shape[1]
    channels = conv_ext.shape[2]
    out_bins = (in_bins - 3) // 2 + 1
    running = jnp.zeros((out_frames * out_bins, channels), jnp.float32)
    for row_tap in range(3):
        tap_rows = lax.slice(conv_ext, (row_tap, 0, 0), (row_tap + 2 * out_frames - 1, in_bins, channels), (2, 1, 1))
        if row_tap == 0:
            tap_rows = tap_rows * keep_left[:, None, None]
        for mel_tap in range(3):
            window = lax.slice(tap_rows, (0, mel_tap, 0), (out_frames, mel_tap + 2 * out_bins - 1, channels), (1, 2, 1))
            running = running + jnp.dot(window.reshape(out_frames * out_bins, channels), conv2_weight[3 * row_tap + mel_tap], preferred_element_type=jnp.float32)
    return jnp.maximum(running, 0.0).astype(jnp.bfloat16).reshape(out_frames, out_bins * channels)

def depthwise(extended, seg_ext, seg_mid, taps, reverse):
    kernel = taps.shape[0]
    frame_count = seg_mid.shape[0]
    running = jnp.zeros((frame_count, extended.shape[1]), jnp.float32)
    for offset in range(kernel):
        source = kernel - 1 - offset if reverse else offset
        window = extended[source:source + frame_count].astype(jnp.float32)
        same_utt = (seg_ext[source:source + frame_count] == seg_mid).astype(jnp.float32)
        running = running + window * same_utt[:, None] * taps[offset][None, :]
    return running

def reference(loader_frames, block_dest, utt_lengths, conv1_weight, conv2_weight, proj_weight, gain_in, point_in, taps, gain_mid, point_out, grad_encoded):
    seat_rows = jnp.arange(N_SEQ, dtype=jnp.int32)[:, None]
    streams = jnp.zeros_like(loader_frames).at[seat_rows, block_dest].set(loader_frames)
    grouped = streams.reshape(N_SEQ, N_DP, BLK_DEV, BLK * MEL).transpose(1, 0, 2, 3).reshape(N_DP, N_SEQ * BLK_DEV * BLK, MEL)
    half_width = (KERNEL - 1) // 2

    def one_group(inputs):
        raw_frames, lengths, cotangent = inputs
        utt_ends = jnp.cumsum(lengths)
        starts = utt_ends - lengths
        block_ids = jnp.arange(N_SEQ * BLK_DEV, dtype=jnp.int32)
        is_start = jnp.any(block_ids[:, None] == starts[None, :], axis=1)
        raw_ext = jnp.concatenate([jnp.zeros((1, MEL), jnp.bfloat16), raw_frames], axis=0)
        conv_first = first_conv(raw_ext, start_keep(is_start, BLK // 2), conv1_weight)
        conv_ext = jnp.concatenate([jnp.zeros((1,) + conv_first.shape[1:], jnp.bfloat16), conv_first], axis=0)
        features = second_conv(conv_ext, start_keep(is_start, BLK // 4), conv2_weight)
        encoder_in = jnp.dot(features, proj_weight, preferred_element_type=jnp.float32).astype(jnp.bfloat16)
        frame_count = encoder_in.shape[0]
        frame_ids = jnp.arange(frame_count, dtype=jnp.int32) // (BLK // 4)
        seg_mid = lax.optimization_barrier(jnp.sum((frame_ids[:, None] >= utt_ends[None, :]).astype(jnp.int32), axis=1))
        rim_seg = jnp.full((half_width,), -1, jnp.int32)
        seg_ext = jnp.concatenate([rim_seg, seg_mid, rim_seg])
        encoder_f = encoder_in.astype(jnp.float32)
        normed_in, inv_in = layer_norm(encoder_f)
        projected = jnp.dot((normed_in * gain_in).astype(jnp.bfloat16), point_in, preferred_element_type=jnp.float32)
        glu_left = projected[:, :D]
        glu_gate = jax.nn.sigmoid(projected[:, D:])
        glu_out = (glu_left * glu_gate).astype(jnp.bfloat16)
        rim_zero = jnp.zeros((half_width, D), jnp.bfloat16)
        mixed_conv = depthwise(jnp.concatenate([rim_zero, glu_out, rim_zero], axis=0), seg_ext, seg_mid, taps, False)
        normed_mid, inv_mid = layer_norm(mixed_conv)
        activated, swish_slope = swish_parts(normed_mid * gain_mid)
        hidden = activated.astype(jnp.bfloat16)
        encoded = (encoder_f + jnp.dot(hidden, point_out, preferred_element_type=jnp.float32)).astype(jnp.bfloat16)
        d_hidden = lax.dot_general(cotangent, point_out, (((1,), (1,)), ((), ())), preferred_element_type=jnp.float32)
        d_mixed = norm_back(d_hidden * swish_slope * gain_mid, normed_mid, inv_mid).astype(jnp.bfloat16)
        d_glu = depthwise(jnp.concatenate([rim_zero, d_mixed, rim_zero], axis=0), seg_ext, seg_mid, taps, True)
        d_projected = jnp.concatenate([d_glu * glu_gate, d_glu * glu_left * glu_gate * (1.0 - glu_gate)], axis=1).astype(jnp.bfloat16)
        d_normed = lax.dot_general(d_projected, point_in, (((1,), (1,)), ((), ())), preferred_element_type=jnp.float32)
        grad_input = (cotangent.astype(jnp.float32) + norm_back(d_normed * gain_in, normed_in, inv_in)).astype(jnp.bfloat16)
        return (encoded, grad_input)
    encoded, grad_input = lax.map(one_group, (grouped, utt_lengths, grad_encoded))
    return (encoded, grad_input)
```

```python
import functools

import jax
import jax.numpy as jnp
import numpy as np
from jax import lax
from jax.experimental import pallas as pl
from jax.experimental.pallas import tpu as pltpu
from jax.sharding import PartitionSpec as P

BLK = 8
PITCH = 32
WIDE = BLK * PITCH
MEL_STEP = 20
MEL_LEAD = 4
MEL_KEEP = 27
FULL = 4
BINS = FULL + 1
BINS_IN = 13
BIN_ORDER = tuple(range(0, BINS_IN, 2)) + tuple(range(1, BINS_IN, 2))
EVENS = (BINS_IN + 1) // 2
RIM = 32
F32 = jnp.float32
BF16 = jnp.bfloat16
VMEM = pl.BlockSpec(memory_space=pltpu.VMEM)
SMEM = pl.BlockSpec(memory_space=pltpu.SMEM)
HBM = pl.BlockSpec(memory_space=pltpu.HBM)


def iota(shape, dim):
    return lax.broadcasted_iota(jnp.int32, shape, dim)


def one_hot(condition):
    return jnp.where(condition, 1.0, 0.0).astype(BF16)


def dot(left, right):
    return jnp.dot(left, right, preferred_element_type=F32)


def dot_rows(left, right):
    return lax.dot_general(left, right, (((0,), (0,)), ((), ())), preferred_element_type=F32)


def dot_cols(left, right):
    return lax.dot_general(left, right, (((1,), (1,)), ((), ())), preferred_element_type=F32)


def send_kernel(place_ref, frames_ref, dest_ref, proj_ref, out_ref, same_ref, other_ref):
    group = place_ref[0]
    blocks = frames_ref.shape[0]
    slots = 2 * blocks
    span = pl.multiple_of((group // 2) * 128, 128)
    pair = dest_ref[:, pl.ds(span, 128)]
    pair = jnp.where(group % 2 == 1, pltpu.roll(pair, 128 - blocks, 1), pair)
    row = jnp.broadcast_to(pair, (128, 128)) // blocks
    at_row, at_col = iota((128, 128), 0), iota((128, 128), 1)
    column = jnp.sum(jnp.where(at_row == at_col, row, 0), axis=1, keepdims=True)
    same = (row == column) & (at_row < at_col) & (at_row < blocks)
    rank = jnp.sum(jnp.where(same, 1, 0), axis=0, keepdims=True)
    slot = (row[0:1] * 2 + rank)[:, 0:blocks]
    sorted_blocks = dot(one_hot(iota((slots, blocks), 0) == slot), frames_ref[...])
    out_ref[...] = sorted_blocks.astype(BF16).reshape(out_ref.shape)
    half = same_ref.shape[1]
    left, right = proj_ref[:, 0:half], proj_ref[:, half : 2 * half]
    odd = group % 2 == 1
    same_ref[...] = jnp.where(odd, right, left)
    other_ref[...] = jnp.where(odd, left, right)


def landing_kernel(place_ref, dest_ref, out_ref):
    group = place_ref[0]
    groups, blocks = dest_ref.shape
    slots = 2 * groups
    dest = dest_ref[...]
    mine = dest // blocks == group
    earlier = one_hot(iota((blocks, blocks), 0) < iota((blocks, blocks), 1))
    rank = dot(one_hot(mine), earlier)
    spot = (dest % blocks + 1).astype(F32)
    at_row, at_col = iota((slots, groups), 0), iota((slots, groups), 1)
    landing = jnp.zeros((slots, blocks), F32)
    for copy in range(2):
        kept = jnp.where(mine & (rank == float(copy)), spot, 0.0).astype(BF16)
        landing = landing + dot(one_hot(at_row == 2 * at_col + copy), kept)
    landing = jnp.sum(landing, axis=1, keepdims=True).astype(jnp.int32) - 1
    out_ref[...] = one_hot(iota((slots, blocks), 1) == landing)


def place_kernel(place_ref, arrived_ref, landing_ref, cut_ref, cot_ref, out_ref):
    group, seat = place_ref[0], place_ref[1]
    blocks = landing_ref.shape[1]
    seats = out_ref.shape[0]
    arrived = arrived_ref[...].reshape(landing_ref.shape[0], arrived_ref.shape[2])
    placed = dot_rows(landing_ref[...], arrived).astype(BF16)
    windows = dot(placed, cut_ref[...])
    pieces = (out_ref.shape[1] - blocks) // 16
    count = cot_ref.shape[0]
    for share in range(seats):
        target = share ^ (group // 16)
        window = windows[:, share * WIDE : (share + 1) * WIDE]
        out_ref[target, 0:blocks, :] = window.astype(BF16)
        for piece in range(pieces):
            columns = slice(piece * WIDE, (piece + 1) * WIDE)
            tail = cot_ref[count - 16 : count, columns]
            head = cot_ref[0:16, columns]
            edge = jnp.where(seat + 1 == target, tail.astype(F32), head.astype(F32))
            out_ref[target, blocks + 16 * piece : blocks + 16 * piece + 16, :] = edge.astype(BF16)


def row_starts(share):
    start_a = jnp.where(share == 0, 2176, jnp.where(share == 2, 128, 0))
    start_b = jnp.where(share == 1, 2304, jnp.where(share == 3, 256, 2432))
    return 128 * share + 128, start_a, start_b


def proj_copies(core, same_hbm, other_hbm, proj_ref, sems):
    rows, half = same_hbm.shape
    pairs = []
    for here in range(2):
        sources = (same_hbm, other_hbm) if here == 0 else (other_hbm, same_hbm)
        pairs.append(
            [
                pltpu.make_async_copy(
                    sources[part],
                    proj_ref.at[pl.ds(128, rows), pl.ds(part * half, half)],
                    sems.at[part],
                )
                for part in range(2)
            ]
        )

    def start():
        for here in range(2):

            @pl.when(core == here)
            def _():
                for copy in pairs[here]:
                    copy.start()

    def wait():
        for copy in pairs[0]:
            copy.wait()

    return start, wait


def project(features, share, proj_ref):
    start, start_a, start_b = row_starts(share)
    result = None
    for index in range(FULL + 2):
        if index < FULL:
            at, size, column = start + 512 * index, 512, 512 * index
        else:
            at, size = (start_a, 256) if index == FULL else (start_b, 256)
            column = 512 * FULL + 256 * (index - FULL)
        weight = proj_ref[pl.ds(pl.multiple_of(at, 128), size), :]
        part = dot(features(column, size), weight)
        result = part if result is None else result + part
    return result


def zero_rims(proj_ref, rows):
    rim = jnp.zeros((128, proj_ref.shape[1]), BF16)
    proj_ref[0:128, :] = rim
    proj_ref[128 + rows : 256 + rows, :] = rim


def conv_kernel(fused, place_ref, chunk_ref, lengths_ref, blocks_ref, conv1_ref, conv2_hbm, *refs):
    group, seat = place_ref[0], place_ref[1]
    share = seat ^ (group // 16)
    if fused:
        same_hbm, other_hbm, out_ref, conv2_ref, patch_ref, first_ref, total_ref = refs[:7]
        conv2_sems, proj_ref, proj_sems = refs[7:]
        proj_start, proj_wait = proj_copies(group % 2, same_hbm, other_hbm, proj_ref, proj_sems)
    else:
        out_ref, conv2_ref, patch_ref, first_ref, total_ref, conv2_sems = refs
    taps, channels = conv2_ref.shape[0], conv2_ref.shape[1]
    frames = out_ref.shape[0]
    conv2_copies = [
        pltpu.make_async_copy(conv2_hbm.at[tap], conv2_ref.at[tap], conv2_sems.at[tap])
        for tap in range(taps)
    ]
    for copy in conv2_copies:
        copy.start()
    if fused:
        proj_start()
    windows = jnp.concatenate([blocks_ref[index, 0:64, :] for index in range(4)], axis=0)
    count = windows.shape[0]
    frame = (chunk_ref[0] * 128 + iota((frames, count), 0)) % (2 * count)
    block = iota((frames, count), 1)
    own_block = frame // 2
    second = lengths_ref[0]
    third = second + lengths_ref[1]
    begins = (own_block == 0) | (own_block == second) | (own_block == third)
    odd = frame % 2 == 1
    here = own_block == block
    before = (own_block - 1 == block) & jnp.logical_not(begins)
    here_odd = dot(one_hot(odd & here), windows)
    here_even = dot(one_hot(jnp.logical_not(odd) & here), windows)
    prev_even = dot(one_hot(jnp.logical_not(odd) & before), windows)
    lane = iota((frames, WIDE), 1)
    patches = pltpu.roll(here_odd, WIDE - PITCH, 1) + pltpu.roll(
        jnp.where(lane < 5 * PITCH, here_even, prev_even), 3 * PITCH, 1
    )
    for index, mel_bin in enumerate(BIN_ORDER):
        moved = patches if mel_bin == 0 else pltpu.roll(patches, WIDE - 2 * mel_bin, 1)
        patch_ref[index * frames : (index + 1) * frames, :] = moved.astype(BF16)
    tap_lane, tap_at = iota((WIDE, 16), 0), iota((WIDE, 16), 1)
    all_rows = BINS_IN * frames
    for row_tap in range(3):
        spread = (2 * row_tap + tap_at // 3) * PITCH + tap_at % 3
        weight = dot(one_hot((tap_lane == spread) & (tap_at < 9)), conv1_ref[...]).astype(BF16)
        for start in range(0, all_rows, 512):
            stop = min(start + 512, all_rows)
            response = dot(patch_ref[start:stop, :], weight)
            first_ref[row_tap, start:stop, :] = jnp.maximum(response, 0.0).astype(BF16)
    if fused:
        zero_rims(proj_ref, same_hbm.shape[0])
    whole_rows = (1, EVENS + 1, 2)
    half_rows = (0, EVENS, 1)
    bin_a = jnp.where(share == 0, 5, 0)
    bin_b = jnp.where(share == 3, 0, 5)
    side_a = jnp.where((share == 1) | (share == 2), 1, 0)
    side_b = jnp.where((share == 0) | (share == 3), 1, 0)
    half = channels // 2
    for tap in range(taps):
        conv2_copies[tap].wait()
        row_tap, mel_tap = tap // 3, tap % 3
        for part in range(FULL):
            at = (whole_rows[mel_tap] + part) * frames
            product = dot(first_ref[row_tap, at : at + frames, :], conv2_ref[tap])
            rows = slice(part * frames, (part + 1) * frames)
            if tap == 0:
                total_ref[rows, :] = product
            else:
                total_ref[rows, :] += product
        rows = slice(FULL * frames, BINS * frames)
        for index, (mel_bin, side) in enumerate(((bin_a, side_a), (bin_b, side_b))):
            at = pl.multiple_of((half_rows[mel_tap] + mel_bin) * frames, 128)
            columns = pl.ds(pl.multiple_of(side * half, 128), half)
            product = dot(
                first_ref[row_tap, pl.ds(at, frames), :], conv2_ref[tap, :, columns]
            )
            columns = slice(index * half, (index + 1) * half)
            if tap == 0:
                total_ref[rows, columns] = product
            else:
                total_ref[rows, columns] += product
    if fused:
        proj_wait()

        def features(column, size):
            mel_bin, inside = column // channels, column % channels
            feature = total_ref[mel_bin * frames : (mel_bin + 1) * frames, inside : inside + size]
            return jnp.maximum(feature, 0.0).astype(BF16)

        out_ref[...] = project(features, share, proj_ref).astype(BF16)
    else:
        for mel_bin in range(BINS):
            feature = total_ref[mel_bin * frames : (mel_bin + 1) * frames, :]
            columns = slice(mel_bin * channels, (mel_bin + 1) * channels)
            out_ref[:, columns] = jnp.maximum(feature, 0.0).astype(BF16)


def conv_chunk(place, chunk, lengths, blocks, conv1_weight, conv2_weight, frames, proj=()):
    taps, channels, _ = conv2_weight.shape
    fused = len(proj) > 0
    width = 2 * proj[0].shape[1] if fused else BINS * channels
    scratch = [
        pltpu.VMEM(conv2_weight.shape, BF16),
        pltpu.VMEM((BINS_IN * frames, WIDE), BF16),
        pltpu.VMEM((3, BINS_IN * frames, channels), BF16),
        pltpu.VMEM((BINS * frames, channels), F32),
        pltpu.SemaphoreType.DMA((taps,)),
    ]
    if fused:
        rows = proj[0].shape[0] + 256
        scratch += [pltpu.VMEM((rows, width), BF16), pltpu.SemaphoreType.DMA((2,))]
    call = pl.pallas_call(
        functools.partial(conv_kernel, fused),
        out_shape=jax.ShapeDtypeStruct((frames, width), BF16),
        in_specs=[SMEM, SMEM, SMEM, VMEM, VMEM, HBM] + [HBM] * len(proj),
        out_specs=VMEM,
        scratch_shapes=scratch,
        compiler_params=pltpu.CompilerParams(vmem_limit_bytes=56 * 1024 * 1024),
        name="conv_fused" if fused else "conv_plain",
    )
    return call(place, chunk, lengths, blocks, conv1_weight, conv2_weight, *proj)


def proj_kernel(place_ref, features_ref, same_hbm, other_hbm, out_ref, proj_ref, proj_sems):
    group, seat = place_ref[0], place_ref[1]
    start, wait = proj_copies(group % 2, same_hbm, other_hbm, proj_ref, proj_sems)
    start()
    zero_rims(proj_ref, same_hbm.shape[0])
    wait()

    def features(column, size):
        return features_ref[:, column : column + size]

    out_ref[...] = project(features, seat ^ (group // 16), proj_ref).astype(BF16)


def projected_chunks(place, features, proj):
    rows, half = proj[0].shape
    return pl.pallas_call(
        proj_kernel,
        out_shape=jax.ShapeDtypeStruct((features.shape[0], 2 * half), BF16),
        in_specs=[SMEM, VMEM, HBM, HBM],
        out_specs=VMEM,
        scratch_shapes=[
            pltpu.VMEM((rows + 256, 2 * half), BF16),
            pltpu.SemaphoreType.DMA((2,)),
        ],
        compiler_params=pltpu.CompilerParams(vmem_limit_bytes=48 * 1024 * 1024),
        name="projection",
    )(place, features, *proj)


def layer_norm(values):
    average = jnp.mean(values, axis=-1, keepdims=True)
    centered = values - average
    inverse = lax.rsqrt(jnp.mean(centered * centered, axis=-1, keepdims=True) + 1e-05)
    return centered * inverse, inverse


def norm_back(d_normed, normed, inverse):
    return (
        d_normed
        - jnp.mean(d_normed, axis=-1, keepdims=True)
        - normed * jnp.mean(d_normed * normed, axis=-1, keepdims=True)
    ) * inverse


def depthwise(source_ref, seg_ref, taps_ref, out_ref, base, seg_base, count, reverse):
    kernel, width = taps_ref.shape
    half = (kernel - 1) // 2
    step = 32
    for begin in range(0, count, step):
        mine = seg_ref[seg_base + begin : seg_base + begin + step, :]
        running = [jnp.zeros((step, 128), F32) for _ in range(width // 128)]
        for offset in range(kernel):
            shift = half - offset if reverse else offset - half
            other = seg_base + begin + shift
            same = seg_ref[other : other + step, :] == mine
            at = base + begin + shift
            for index in range(width // 128):
                lanes = slice(index * 128, (index + 1) * 128)
                window = jnp.where(same, source_ref[at : at + step, lanes], 0.0)
                running[index] = running[index] + window * taps_ref[offset : offset + 1, lanes]
        for index in range(width // 128):
            out_ref[begin : begin + step, index * 128 : (index + 1) * 128] = running[index]


def module_kernel(
    place_ref,
    lengths_ref,
    low_ref,
    own_ref,
    high_ref,
    cot_low_ref,
    cot_ref,
    cot_high_ref,
    gain_in_ref,
    point_in_ref,
    taps_ref,
    gain_mid_ref,
    point_out_ref,
    encoded_ref,
    grad_ref,
    glu_ref,
    seg_ref,
    mixed_ref,
    back_ref,
):
    own = own_ref.shape[0]
    width = own_ref.shape[1]
    half = (taps_ref.shape[0] - 1) // 2
    total = own + 2 * RIM
    inner = own + RIM
    skip = RIM // 2
    encoder = jnp.concatenate([low_ref[...], own_ref[...], high_ref[...]], axis=0).astype(F32)
    normed_in, inv_in = layer_norm(encoder)
    ln_in = (normed_in * gain_in_ref[...]).astype(BF16)
    left = dot(ln_in, point_in_ref[:, 0:width])
    gate = jax.nn.sigmoid(dot(ln_in, point_in_ref[:, width : 2 * width]))
    glu_ref[...] = (left * gate).astype(BF16).astype(F32)
    frame = place_ref[1] * own - RIM + iota((total, 128), 0)
    block = (frame + 4 * RIM) // 2 - 2 * RIM
    second = lengths_ref[0]
    third = second + lengths_ref[1]
    ends = third + lengths_ref[2]
    seg = (
        jnp.where(block >= 0, 1, 0)
        + jnp.where(block >= second, 1, 0)
        + jnp.where(block >= third, 1, 0)
        + jnp.where(block >= ends, 1, 0)
    )
    seg_ref[...] = seg
    depthwise(glu_ref, seg_ref, taps_ref, mixed_ref, skip, skip, inner, False)
    normed_mid, inv_mid = layer_norm(mixed_ref[...])
    scaled = normed_mid * gain_mid_ref[...]
    logistic = jax.nn.sigmoid(scaled)
    slope = logistic * (1.0 + scaled * (1.0 - logistic))
    low = RIM - skip
    hidden = (scaled * logistic)[low : low + own].astype(BF16)
    encoded = encoder[RIM : RIM + own] + dot(hidden, point_out_ref[...])
    encoded_ref[...] = encoded.astype(BF16)
    cotangent = jnp.concatenate([cot_low_ref[...], cot_ref[...], cot_high_ref[...]], axis=0)
    d_hidden = dot_cols(cotangent, point_out_ref[...])
    d_mixed = norm_back(d_hidden * slope * gain_mid_ref[...], normed_mid, inv_mid)
    mixed_ref[...] = d_mixed.astype(BF16).astype(F32)
    depthwise(mixed_ref, seg_ref, taps_ref, back_ref, low, RIM, own, True)
    d_glu = back_ref[...]
    own_gate = gate[RIM : RIM + own]
    d_left = d_glu * own_gate
    d_right = d_left * left[RIM : RIM + own] * (1.0 - own_gate)
    d_normed = dot_cols(d_left.astype(BF16), point_in_ref[:, 0:width])
    d_normed = d_normed + dot_cols(d_right.astype(BF16), point_in_ref[:, width : 2 * width])
    own_normed = normed_in[RIM : RIM + own]
    back = norm_back(d_normed * gain_in_ref[...], own_normed, inv_in[RIM : RIM + own])
    grad_ref[...] = (cot_ref[...].astype(F32) + back).astype(BF16)


def conv_module(place, lengths, parts, cotangents, gain_in, point_in, taps, gain_mid, point_out):
    own, width = parts[1].shape
    inner = own + RIM
    shape = jax.ShapeDtypeStruct((own, width), BF16)
    return pl.pallas_call(
        module_kernel,
        out_shape=(shape, shape),
        in_specs=[SMEM, SMEM] + [VMEM] * 11,
        out_specs=(VMEM, VMEM),
        scratch_shapes=[
            pltpu.VMEM((own + 2 * RIM, width), F32),
            pltpu.VMEM((own + 2 * RIM, 128), jnp.int32),
            pltpu.VMEM((inner, width), F32),
            pltpu.VMEM((own, width), F32),
        ],
        compiler_params=pltpu.CompilerParams(vmem_limit_bytes=48 * 1024 * 1024),
        name="conv_module",
    )(place, lengths, *parts, *cotangents, gain_in[None], point_in, taps, gain_mid[None], point_out)
def send(place, frames, block_dest, proj_weight):
    blocks, width = frames.shape
    rows, columns = proj_weight.shape
    shape = jax.ShapeDtypeStruct((rows, columns // 2), BF16)
    return pl.pallas_call(
        send_kernel,
        out_shape=(jax.ShapeDtypeStruct((blocks, 2, width), BF16), shape, shape),
        in_specs=[SMEM, VMEM, VMEM, VMEM],
        out_specs=(VMEM, VMEM, VMEM),
        name="send",
    )(place, frames, block_dest, proj_weight)


def landing_slots(place, dest):
    groups, blocks = dest.shape
    return pl.pallas_call(
        landing_kernel,
        out_shape=jax.ShapeDtypeStruct((2 * groups, blocks), BF16),
        in_specs=[SMEM, VMEM],
        out_specs=VMEM,
        name="landing",
    )(place, dest)


def cut_matrix(seats, width):
    mel_bins = width // BLK
    share, frame, mel = np.meshgrid(
        np.arange(seats), np.arange(BLK), np.arange(PITCH), indexing="ij"
    )
    source = MEL_STEP * share - MEL_LEAD + mel
    fits = (mel < MEL_KEEP) & (source >= 0) & (source < mel_bins)
    source = np.where(fits, frame * mel_bins + source, -1).reshape(-1)
    return jnp.asarray(np.arange(width)[:, None] == source[None, :], BF16)


def place_blocks(place, arrived, landing, cotangent, seats):
    rim_rows = 16 * cotangent.shape[1] // WIDE
    return pl.pallas_call(
        place_kernel,
        out_shape=jax.ShapeDtypeStruct((seats, landing.shape[1] + rim_rows, WIDE), BF16),
        in_specs=[SMEM, VMEM, VMEM, VMEM, VMEM],
        out_specs=VMEM,
        name="place",
    )(place, arrived, landing, cut_matrix(seats, arrived.shape[2]), cotangent)


def share_routes(groups, seats, flip):
    cluster = groups // seats
    routes = []
    for group in range(groups):
        for seat in range(seats):
            target = ((group // cluster) ^ seat) * cluster + (group % cluster ^ flip)
            routes.append((group * seats + seat, target * seats + seat))
    return routes


def gather_share(pair, groups, cluster):
    members = [
        [begin + core + 2 * index for index in range(cluster // 2)]
        for begin in range(0, groups, cluster)
        for core in range(2)
    ]
    rows, half = pair.shape
    copies = jnp.broadcast_to(pair[None], (cluster // 2, rows, half))
    same = lax.all_to_all(
        copies, "dp", split_axis=0, concat_axis=0, tiled=True, axis_index_groups=members
    ).reshape(-1, half)
    other = lax.ppermute(same, "dp", [(index, index ^ 1) for index in range(groups)])
    return same, other


def edge_rows(windows, seat, seats, rows, width):
    edge = lax.dynamic_index_in_dim(windows, (seat + seats) % seats, 0, keepdims=False)[-rows:]
    pieces = width // WIDE
    return edge.reshape(pieces, rows // pieces, WIDE).transpose(1, 0, 2).reshape(-1, width)


def local(
    loader_frames,
    block_dest,
    utt_lengths,
    conv1_weight,
    conv2_weight,
    proj_weight,
    gain_in,
    point_in,
    taps,
    gain_mid,
    point_out,
    grad_encoded,
):
    groups, seats = lax.axis_size("dp"), lax.axis_size("seq")
    group, seat = lax.axis_index("dp"), lax.axis_index("seq")
    place = jnp.stack([group, seat]).astype(jnp.int32)
    lengths = utt_lengths[0]
    frames = loader_frames[0]
    blocks = frames.shape[0]
    cotangent = grad_encoded[0]
    own, width = cotangent.shape
    channels = conv2_weight.shape[1]
    rows = proj_weight.shape[0]
    cluster = groups // seats
    half = width // 2
    core = group % 2
    outgoing, same, other = send(place, frames, block_dest, proj_weight)
    same = lax.ppermute(same, ("dp", "seq"), share_routes(groups, seats, 0))
    other = lax.ppermute(other, ("dp", "seq"), share_routes(groups, seats, 1))
    arrived = lax.all_to_all(outgoing, "dp", split_axis=0, concat_axis=0, tiled=True)
    landing = landing_slots(place, block_dest.reshape(groups, blocks))
    pair = jnp.where(
        core == 0,
        jnp.concatenate([same, other], axis=0),
        jnp.concatenate([other, same], axis=0),
    )
    same, other = gather_share(pair, groups, cluster)
    windows = place_blocks(place, arrived, landing, cotangent, seats)
    windows = lax.all_to_all(windows, "seq", split_axis=0, concat_axis=0, tiled=True)
    conv1 = jnp.pad(conv1_weight, ((0, 16 - conv1_weight.shape[0]), (0, 0)))

    def chunk_at(step):
        return ((seat + step) % seats).reshape(1).astype(jnp.int32)

    def ring(step):
        return [(index, (index + step) % seats) for index in range(seats)]

    far = conv_chunk(place, chunk_at(1), lengths, windows, conv1, conv2_weight, 3 * own)
    far = projected_chunks(place, far, (same, other))
    from_two = lax.ppermute(far[own : 2 * own], "seq", ring(2))
    from_one = lax.ppermute(far[:own], "seq", ring(1))
    from_three = lax.ppermute(far[2 * own :], "seq", ring(3))
    mine = conv_chunk(
        place, chunk_at(0), lengths, windows, conv1, conv2_weight, own, (same, other)
    )
    total = from_two.astype(F32) + from_one.astype(F32)
    total = total + from_three.astype(F32) + mine.astype(F32)
    encoder_in = total.astype(BF16)
    low = lax.ppermute(encoder_in[-RIM:], "seq", ring(1))
    high = lax.ppermute(encoder_in[:RIM], "seq", ring(3))
    rim_rows = 16 * width // WIDE
    cot_low = edge_rows(windows, seat - 1, seats, rim_rows, width)
    cot_high = edge_rows(windows, seat + 1, seats, rim_rows, width)
    encoded, grad_input = conv_module(
        place,
        lengths,
        (low, encoder_in, high),
        (cot_low, cotangent, cot_high),
        gain_in,
        point_in,
        taps,
        gain_mid,
        point_out,
    )
    return encoded[None], grad_input[None]


def solution(mesh):
    placed = (
        P("seq", "dp", None),
        P("seq", None),
        P("dp", None),
        P(),
        P(),
        P("dp", None),
        P(),
        P(),
        P(),
        P(),
        P(),
        P("dp", "seq", None),
    )
    return jax.shard_map(
        local,
        mesh=mesh,
        in_specs=placed,
        out_specs=(P("dp", "seq", None), P("dp", "seq", None)),
        check_vma=False,
    )
```

```python
import functools

import jax
import jax.numpy as jnp
import numpy as np
from jax import lax
from jax.experimental import pallas as pl
from jax.experimental.pallas import tpu as pltpu
from jax.sharding import PartitionSpec as P

BLK = 8
PITCH = 32
WIDE = BLK * PITCH
MEL_STEP = 20
MEL_LEAD = 4
MEL_KEEP = 27
FULL = 4
BINS = FULL + 1
BINS_IN = 13
BIN_ORDER = tuple(range(0, BINS_IN, 2)) + tuple(range(1, BINS_IN, 2))
EVENS = (BINS_IN + 1) // 2
RIM = 32
PROJ_PARTS = 4
CONV_ROWS = 256
F32 = jnp.float32
BF16 = jnp.bfloat16
VMEM = pl.BlockSpec(memory_space=pltpu.VMEM)
SMEM = pl.BlockSpec(memory_space=pltpu.SMEM)
HBM = pl.BlockSpec(memory_space=pltpu.HBM)


def iota(shape, dim):
    return lax.broadcasted_iota(jnp.int32, shape, dim)


def one_hot(condition):
    return jnp.where(condition, 1.0, 0.0).astype(BF16)


def dot(left, right):
    return jnp.dot(left, right, preferred_element_type=F32)


def dot_rows(left, right):
    return lax.dot_general(left, right, (((0,), (0,)), ((), ())), preferred_element_type=F32)


def dot_cols(left, right):
    return lax.dot_general(left, right, (((1,), (1,)), ((), ())), preferred_element_type=F32)


def send_kernel(place_ref, frames_ref, dest_ref, proj_ref, out_ref, same_ref, other_ref):
    group = place_ref[0]
    blocks = frames_ref.shape[0]
    span = pl.multiple_of((group // 2) * 128, 128)
    pair = dest_ref[:, pl.ds(span, 128)]
    pair = jnp.where(group % 2 == 1, pltpu.roll(pair, 128 - blocks, 1), pair)
    row = jnp.broadcast_to(pair, (128, 128)) // blocks
    at_row, at_col = iota((128, 128), 0), iota((128, 128), 1)
    column = jnp.sum(jnp.where(at_row == at_col, row, 0), axis=1, keepdims=True)
    same = (row == column) & (at_row < at_col) & (at_row < blocks)
    rank = jnp.sum(jnp.where(same, 1, 0), axis=0, keepdims=True)
    slot = (row[0:1] * 2 + rank)[:, 0:blocks]
    sorted_blocks = dot(one_hot(iota((2 * blocks, blocks), 0) == slot), frames_ref[...])
    out_ref[...] = sorted_blocks.astype(BF16).reshape(out_ref.shape)
    half = same_ref.shape[1]
    left, right = proj_ref[:, 0:half], proj_ref[:, half : 2 * half]
    odd = group % 2 == 1
    same_ref[...] = jnp.where(odd, right, left)
    other_ref[...] = jnp.where(odd, left, right)


def landing_kernel(place_ref, dest_ref, out_ref):
    group = place_ref[0]
    groups, blocks = dest_ref.shape
    dest = dest_ref[...]
    mine = dest // blocks == group
    earlier = one_hot(iota((blocks, blocks), 0) < iota((blocks, blocks), 1))
    rank = dot(one_hot(mine), earlier)
    spot = dest % blocks
    for copy in range(2):
        kept = jnp.where(mine & (rank == float(copy)), spot + 1, 0)
        landing = jnp.sum(kept, axis=1, keepdims=True) - 1
        out_ref[copy] = one_hot(iota((groups, blocks), 1) == landing)


def place_kernel(place_ref, arrived_ref, landing_ref, cut_ref, cot_ref, *out_refs):
    group, seat = place_ref[0], place_ref[1]
    window_ref = out_refs[-1]
    blocks = landing_ref.shape[2]
    arrived = arrived_ref[...]
    placed = dot_rows(landing_ref[0], arrived[:, 0, :]) + dot_rows(
        landing_ref[1], arrived[:, 1, :]
    )
    seats = len(out_refs) - 1
    window_ref[...] = dot(placed.astype(BF16), cut_ref[...]).astype(BF16)
    count = cot_ref.shape[0]
    for step in range(seats):
        share = ((seat + step) % seats) ^ (group // 16)
        span = pl.ds(pl.multiple_of(share * WIDE, WIDE), WIDE)
        out_refs[step][0:blocks, :] = window_ref[:, span]
        if step in (1, seats - 1):
            begin = count - 16 if step == 1 else 0
            for piece in range(cot_ref.shape[1] // WIDE):
                columns = slice(piece * WIDE, (piece + 1) * WIDE)
                rows = slice(blocks + 16 * piece, blocks + 16 * piece + 16)
                out_refs[step][rows, :] = cot_ref[begin : begin + 16, columns]


def row_starts(share):
    start_a = jnp.where(share == 0, 2176, jnp.where(share == 2, 128, 0))
    start_b = jnp.where(share == 1, 2304, jnp.where(share == 3, 256, 2432))
    return 128 * share + 128, start_a, start_b


def proj_copies(core, same_hbm, other_hbm, proj_ref, sems):
    rows, half = same_hbm.shape
    parts = sems.shape[0] // 2
    size = rows // parts

    def copy(here, part, side):
        source = same_hbm if here == side else other_hbm
        return pltpu.make_async_copy(
            source.at[pl.ds(part * size, size)],
            proj_ref.at[pl.ds(128 + part * size, size), pl.ds(side * half, half)],
            sems.at[2 * part + side],
        )

    def start():
        for here in range(2):

            @pl.when(core == here)
            def _():
                for part in range(parts):
                    for side in range(2):
                        copy(here, part, side).start()

    def wait(part):
        for side in range(2):
            copy(0, part, side).wait()

    return start, wait


def project(features, share, proj_ref, wait):
    start, start_a, start_b = row_starts(share)
    result = None
    wait(0)
    for index in range(FULL + 2):
        if index < PROJ_PARTS - 1:
            wait(index + 1)
        if index < FULL:
            at, size, column = start + 512 * index, 512, 512 * index
        else:
            at, size = (start_a, 256) if index == FULL else (start_b, 256)
            column = 512 * FULL + 256 * (index - FULL)
        weight = proj_ref[pl.ds(pl.multiple_of(at, 128), size), :]
        part = dot(features(column, size), weight)
        result = part if result is None else result + part
    return result


def zero_rims(proj_ref, rows):
    rim = jnp.zeros((128, proj_ref.shape[1]), BF16)
    proj_ref[0:128, :] = rim
    proj_ref[128 + rows : 256 + rows, :] = rim


def conv_kernel(place_ref, lengths_ref, *refs):
    block_refs, (conv1_ref, conv2_hbm), refs = refs[:4], refs[4:6], refs[6:]
    out_ref, conv2_ref, patch_ref, first_ref, conv2_sems = refs
    group, seat = place_ref[0], place_ref[1]
    share = seat ^ (group // 16)
    taps, channels = conv2_ref.shape[0], conv2_ref.shape[1]
    frames = out_ref.shape[0]
    conv2_copies = [
        pltpu.make_async_copy(conv2_hbm.at[tap], conv2_ref.at[tap], conv2_sems.at[tap])
        for tap in range(taps)
    ]
    for copy in conv2_copies:
        copy.start()
    windows = jnp.concatenate([block_ref[0:64, :] for block_ref in block_refs], axis=0)
    count = windows.shape[0]
    frame = (seat * 128 + iota((frames, count), 0)) % (2 * count)
    block = iota((frames, count), 1)
    block = ((seat + 4 - block // 64) % 4) * 64 + block % 64
    own_block = frame // 2
    second = lengths_ref[0]
    third = second + lengths_ref[1]
    begins = (own_block == 0) | (own_block == second) | (own_block == third)
    odd = frame % 2 == 1
    here = own_block == block
    before = (own_block - 1 == block) & jnp.logical_not(begins)
    here_odd = dot(one_hot(odd & here), windows)
    here_even = dot(one_hot(jnp.logical_not(odd) & here), windows)
    prev_even = dot(one_hot(jnp.logical_not(odd) & before), windows)
    lane = iota((frames, WIDE), 1)
    patches = pltpu.roll(here_odd, WIDE - PITCH, 1) + pltpu.roll(
        jnp.where(lane < 5 * PITCH, here_even, prev_even), 3 * PITCH, 1
    )
    for index, mel_bin in enumerate(BIN_ORDER):
        moved = patches if mel_bin == 0 else pltpu.roll(patches, WIDE - 2 * mel_bin, 1)
        patch_ref[index * frames : (index + 1) * frames, :] = moved.astype(BF16)
    tap_lane, tap_at = iota((WIDE, 16), 0), iota((WIDE, 16), 1)
    all_rows = BINS_IN * frames
    for row_tap in range(3):
        spread = (2 * row_tap + tap_at // 3) * PITCH + tap_at % 3
        weight = dot(one_hot((tap_lane == spread) & (tap_at < 9)), conv1_ref[...]).astype(BF16)
        for start in range(0, all_rows, 512):
            stop = min(start + 512, all_rows)
            response = dot(patch_ref[start:stop, :], weight)
            first_ref[row_tap, start:stop, :] = jnp.maximum(response, 0.0).astype(BF16)
    whole_rows = (1, EVENS + 1, 2)
    half_rows = (0, EVENS, 1)
    bin_a = jnp.where(share == 0, 5, 0)
    bin_b = jnp.where(share == 3, 0, 5)
    side_a = jnp.where((share == 1) | (share == 2), 1, 0)
    side_b = jnp.where((share == 0) | (share == 3), 1, 0)
    half = channels // 2
    for copy in conv2_copies:
        copy.wait()
    for begin in range(0, frames, CONV_ROWS):
        for part in range(FULL):
            total = None
            for tap in range(taps):
                at = (whole_rows[tap % 3] + part) * frames + begin
                product = dot(first_ref[tap // 3, at : at + CONV_ROWS, :], conv2_ref[tap])
                total = product if total is None else total + product
            columns = slice(part * channels, (part + 1) * channels)
            out_ref[begin : begin + CONV_ROWS, columns] = jnp.maximum(total, 0.0).astype(BF16)
        for index, (mel_bin, side) in enumerate(((bin_a, side_a), (bin_b, side_b))):
            columns = pl.ds(pl.multiple_of(side * half, 128), half)
            total = None
            for tap in range(taps):
                at = (half_rows[tap % 3] + mel_bin) * frames + begin
                rows = pl.ds(pl.multiple_of(at, 128), CONV_ROWS)
                product = dot(first_ref[tap // 3, rows, :], conv2_ref[tap, :, columns])
                total = product if total is None else total + product
            first = FULL * channels + index * half
            columns = slice(first, first + half)
            out_ref[begin : begin + CONV_ROWS, columns] = jnp.maximum(total, 0.0).astype(BF16)


def conv_features(place, lengths, blocks, conv1_weight, conv2_weight, frames):
    taps, channels, _ = conv2_weight.shape
    return pl.pallas_call(
        conv_kernel,
        out_shape=jax.ShapeDtypeStruct((frames, BINS * channels), BF16),
        in_specs=[SMEM] * 2 + [VMEM] * 5 + [HBM],
        out_specs=VMEM,
        scratch_shapes=[
            pltpu.VMEM(conv2_weight.shape, BF16),
            pltpu.VMEM((BINS_IN * frames, WIDE), BF16),
            pltpu.VMEM((3, BINS_IN * frames, channels), BF16),
            pltpu.SemaphoreType.DMA((taps,)),
        ],
        compiler_params=pltpu.CompilerParams(vmem_limit_bytes=48 * 1024 * 1024),
        name="convolutions",
    )(place, lengths, *blocks, conv1_weight, conv2_weight)


def proj_kernel(place_ref, features_ref, same_hbm, other_hbm, *refs):
    out_refs, (result_ref, proj_ref, sems) = refs[:-3], refs[-3:]
    group, seat = place_ref[0], place_ref[1]
    start, wait = proj_copies(group % 2, same_hbm, other_hbm, proj_ref, sems)
    start()
    zero_rims(proj_ref, same_hbm.shape[0])

    def features(column, size):
        return features_ref[:, column : column + size]

    result = project(features, seat ^ (group // 16), proj_ref, wait)
    result_ref[...] = result.astype(BF16)
    count = result_ref.shape[0]
    own = count // len(out_refs)
    for step, out_ref in enumerate(out_refs):
        for at in range(0, own + 2 * RIM, RIM):
            source = (step * own - RIM + at) % count
            out_ref[at : at + RIM, :] = result_ref[source : source + RIM, :]


def projected_chunks(place, features, proj, seats):
    rows, half = proj[0].shape
    frames = features.shape[0]
    shape = jax.ShapeDtypeStruct((frames // seats + 2 * RIM, 2 * half), BF16)
    return pl.pallas_call(
        proj_kernel,
        out_shape=[shape] * seats,
        in_specs=[SMEM, VMEM, HBM, HBM],
        out_specs=[VMEM] * seats,
        scratch_shapes=[
            pltpu.VMEM((frames, 2 * half), BF16),
            pltpu.VMEM((rows + 256, 2 * half), BF16),
            pltpu.SemaphoreType.DMA((2 * PROJ_PARTS,)),
        ],
        compiler_params=pltpu.CompilerParams(vmem_limit_bytes=40 * 1024 * 1024),
        name="projection",
    )(place, features, *proj)


def layer_norm(values):
    average = jnp.mean(values, axis=-1, keepdims=True)
    centered = values - average
    inverse = lax.rsqrt(jnp.mean(centered * centered, axis=-1, keepdims=True) + 1e-05)
    return centered * inverse, inverse


def norm_back(d_normed, normed, inverse):
    return (
        d_normed
        - jnp.mean(d_normed, axis=-1, keepdims=True)
        - normed * jnp.mean(d_normed * normed, axis=-1, keepdims=True)
    ) * inverse


def depthwise(source, seg_ref, taps_ref, moved_ref, out_ref, base, seg_base, count, reverse):
    kernel, width = taps_ref.shape
    half = (kernel - 1) // 2
    length = source.shape[0]
    for residue in range(8):
        for index in range(width // 128):
            lanes = slice(index * 128, (index + 1) * 128)
            column = source[:, lanes]
            if residue:
                column = pltpu.roll(column, length - residue, 0)
            moved_ref[residue, 0:length, lanes] = column
    step = 32
    for begin in range(0, count, step):
        mine = seg_ref[0, seg_base + begin : seg_base + begin + step, :]
        running = [jnp.zeros((step, 128), F32) for _ in range(width // 128)]
        for offset in range(kernel):
            shift = half - offset if reverse else offset - half
            residue = shift % 8
            other = seg_base + begin + shift - residue
            same = seg_ref[residue, other : other + step, :] == mine
            at = base + begin + shift - residue
            for index in range(width // 128):
                lanes = slice(index * 128, (index + 1) * 128)
                window = jnp.where(same, moved_ref[residue, at : at + step, lanes], 0.0)
                running[index] = running[index] + window * taps_ref[offset : offset + 1, lanes]
        for index in range(width // 128):
            out_ref[begin : begin + step, index * 128 : (index + 1) * 128] = running[index]


def module_kernel(
    place_ref,
    lengths_ref,
    part_0_ref,
    part_1_ref,
    part_2_ref,
    part_3_ref,
    cot_low_ref,
    cot_ref,
    cot_high_ref,
    gain_in_ref,
    point_in_ref,
    taps_ref,
    gain_mid_ref,
    point_out_ref,
    encoded_ref,
    grad_ref,
    glu_ref,
    seg_ref,
    mixed_ref,
    back_ref,
):
    own, width = cot_ref.shape
    total = own + 2 * RIM
    inner = own + RIM
    skip = RIM // 2
    encoder = part_0_ref[...].astype(F32) + part_1_ref[...].astype(F32)
    encoder = encoder + part_2_ref[...].astype(F32) + part_3_ref[...].astype(F32)
    encoder = encoder.astype(BF16).astype(F32)
    normed_in, inv_in = layer_norm(encoder)
    ln_in = (normed_in * gain_in_ref[...]).astype(BF16)
    left = dot(ln_in, point_in_ref[:, 0:width])
    gate = jax.nn.sigmoid(dot(ln_in, point_in_ref[:, width : 2 * width]))
    glu_out = (left * gate).astype(BF16).astype(F32)
    frame = place_ref[1] * own - RIM + iota((total, 128), 0)
    block = (frame + 4 * RIM) // 2 - 2 * RIM
    second = lengths_ref[0]
    third = second + lengths_ref[1]
    ends = third + lengths_ref[2]
    seg = (
        jnp.where(block >= 0, 1, 0)
        + jnp.where(block >= second, 1, 0)
        + jnp.where(block >= third, 1, 0)
        + jnp.where(block >= ends, 1, 0)
    )
    for residue in range(8):
        seg_ref[residue] = pltpu.roll(seg, total - residue, 0) if residue else seg
    depthwise(glu_out, seg_ref, taps_ref, glu_ref, mixed_ref, skip, skip, inner, False)
    normed_mid, inv_mid = layer_norm(mixed_ref[...])
    scaled = normed_mid * gain_mid_ref[...]
    logistic = jax.nn.sigmoid(scaled)
    slope = logistic * (1.0 + scaled * (1.0 - logistic))
    low = RIM - skip
    hidden = (scaled * logistic)[low : low + own].astype(BF16)
    encoded = encoder[RIM : RIM + own] + dot(hidden, point_out_ref[...])
    encoded_ref[...] = encoded.astype(BF16)
    low_edge, high_edge = [
        jnp.concatenate([ref[64 + 16 * piece : 80 + 16 * piece, :] for piece in range(3)], axis=1)
        for ref in (cot_low_ref, cot_high_ref)
    ]
    cotangent = jnp.concatenate([low_edge, cot_ref[...], high_edge], axis=0)
    d_hidden = dot_cols(cotangent, point_out_ref[...])
    d_mixed = norm_back(d_hidden * slope * gain_mid_ref[...], normed_mid, inv_mid)
    d_mixed = d_mixed.astype(BF16).astype(F32)
    depthwise(d_mixed, seg_ref, taps_ref, glu_ref, back_ref, low, RIM, own, True)
    d_glu = back_ref[...]
    own_gate = gate[RIM : RIM + own]
    d_left = d_glu * own_gate
    d_right = d_left * left[RIM : RIM + own] * (1.0 - own_gate)
    d_normed = dot_cols(d_left.astype(BF16), point_in_ref[:, 0:width])
    d_normed = d_normed + dot_cols(d_right.astype(BF16), point_in_ref[:, width : 2 * width])
    own_normed = normed_in[RIM : RIM + own]
    back = norm_back(d_normed * gain_in_ref[...], own_normed, inv_in[RIM : RIM + own])
    grad_ref[...] = (cot_ref[...].astype(F32) + back).astype(BF16)


def conv_module(place, lengths, parts, cotangents, gain_in, point_in, taps, gain_mid, point_out):
    own, width = cotangents[1].shape
    inner = own + RIM
    shape = jax.ShapeDtypeStruct((own, width), BF16)
    return pl.pallas_call(
        module_kernel,
        out_shape=(shape, shape),
        in_specs=[SMEM, SMEM] + [VMEM] * 12,
        out_specs=(VMEM, VMEM),
        scratch_shapes=[
            pltpu.VMEM((8, own + 2 * RIM, width), F32),
            pltpu.VMEM((8, own + 2 * RIM, 128), jnp.int32),
            pltpu.VMEM((inner, width), F32),
            pltpu.VMEM((own, width), F32),
        ],
        compiler_params=pltpu.CompilerParams(vmem_limit_bytes=48 * 1024 * 1024),
        name="conv_module",
    )(place, lengths, *parts, *cotangents, gain_in[None], point_in, taps, gain_mid[None], point_out)
def send(place, frames, block_dest, proj_weight):
    blocks, width = frames.shape
    rows, columns = proj_weight.shape
    shape = jax.ShapeDtypeStruct((rows, columns // 2), BF16)
    return pl.pallas_call(
        send_kernel,
        out_shape=(jax.ShapeDtypeStruct((blocks, 2, width), BF16), shape, shape),
        in_specs=[SMEM, VMEM, VMEM, VMEM],
        out_specs=(VMEM, VMEM, VMEM),
        name="send",
    )(place, frames, block_dest, proj_weight)


def landing_slots(place, dest):
    groups, blocks = dest.shape
    return pl.pallas_call(
        landing_kernel,
        out_shape=jax.ShapeDtypeStruct((2, groups, blocks), BF16),
        in_specs=[SMEM, VMEM],
        out_specs=VMEM,
        name="landing",
    )(place, dest)


def cut_matrix(seats, width):
    mel_bins = width // BLK
    share, frame, mel = np.meshgrid(
        np.arange(seats), np.arange(BLK), np.arange(PITCH), indexing="ij"
    )
    source = MEL_STEP * share - MEL_LEAD + mel
    fits = (mel < MEL_KEEP) & (source >= 0) & (source < mel_bins)
    source = np.where(fits, frame * mel_bins + source, -1).reshape(-1)
    return jnp.asarray(np.arange(width)[:, None] == source[None, :], BF16)


def place_blocks(place, arrived, landing, cotangent, seats):
    blocks = landing.shape[2]
    rim_rows = 16 * cotangent.shape[1] // WIDE
    rows = [blocks + (rim_rows if step in (1, seats - 1) else 0) for step in range(seats)]
    return pl.pallas_call(
        place_kernel,
        out_shape=[jax.ShapeDtypeStruct((count, WIDE), BF16) for count in rows],
        in_specs=[SMEM, VMEM, VMEM, VMEM, VMEM],
        out_specs=[VMEM] * seats,
        scratch_shapes=[pltpu.VMEM((blocks, seats * WIDE), BF16)],
        name="place",
    )(place, arrived, landing, cut_matrix(seats, arrived.shape[2]), cotangent)


def share_routes(groups, seats, flip):
    cluster = groups // seats
    routes = []
    for group in range(groups):
        for seat in range(seats):
            target = ((group // cluster) ^ seat) * cluster + (group % cluster ^ flip)
            routes.append((group * seats + seat, target * seats + seat))
    return routes


def gather_share(pair, groups, cluster):
    members = [
        [begin + core + 2 * index for index in range(cluster // 2)]
        for begin in range(0, groups, cluster)
        for core in range(2)
    ]
    rows, half = pair.shape
    copies = jnp.broadcast_to(pair[None], (cluster // 2, rows, half))
    same = lax.all_to_all(
        copies, "dp", split_axis=0, concat_axis=0, tiled=True, axis_index_groups=members
    ).reshape(-1, half)
    return same


def local(
    loader_frames,
    block_dest,
    utt_lengths,
    conv1_weight,
    conv2_weight,
    proj_weight,
    gain_in,
    point_in,
    taps,
    gain_mid,
    point_out,
    grad_encoded,
):
    groups, seats = lax.axis_size("dp"), lax.axis_size("seq")
    group, seat = lax.axis_index("dp"), lax.axis_index("seq")
    place = jnp.stack([group, seat]).astype(jnp.int32)
    lengths = utt_lengths[0]
    frames = loader_frames[0]
    blocks = frames.shape[0]
    cotangent = grad_encoded[0]
    own, width = cotangent.shape
    channels = conv2_weight.shape[1]
    rows = proj_weight.shape[0]
    cluster = groups // seats
    half = width // 2
    core = group % 2
    outgoing, same, other = send(place, frames, block_dest, proj_weight)
    same = lax.ppermute(same, ("dp", "seq"), share_routes(groups, seats, 0))
    other = lax.ppermute(other, ("dp", "seq"), share_routes(groups, seats, 1))
    arrived = lax.all_to_all(outgoing, "dp", split_axis=0, concat_axis=0, tiled=True)
    landing = landing_slots(place, block_dest.reshape(groups, blocks))
    windows = place_blocks(place, arrived, landing, cotangent, seats)
    pair = jnp.where(
        core == 0,
        jnp.concatenate([same, other], axis=0),
        jnp.concatenate([other, same], axis=0),
    )

    def ring(step):
        return [(index, (index + step) % seats) for index in range(seats)]

    windows = [windows[0]] + [
        lax.ppermute(windows[step], "seq", ring(step)) for step in range(1, seats)
    ]
    pair, _ = lax.optimization_barrier((pair, windows[1]))
    same = gather_share(pair, groups, cluster)
    conv1 = jnp.pad(conv1_weight, ((0, 16 - conv1_weight.shape[0]), (0, 0)))
    features = conv_features(place, lengths, windows, conv1, conv2_weight, seats * own)
    features, same = lax.optimization_barrier((features, same))
    other = lax.ppermute(same, "dp", [(index, index ^ 1) for index in range(groups)])
    parts = projected_chunks(place, features, (same, other), seats)
    parts = [parts[0]] + [
        lax.ppermute(parts[step], "seq", ring(step)) for step in range(1, seats)
    ]
    encoded, grad_input = conv_module(
        place,
        lengths,
        parts,
        (windows[1], cotangent, windows[3]),
        gain_in,
        point_in,
        taps,
        gain_mid,
        point_out,
    )
    return encoded[None], grad_input[None]


def solution(mesh):
    placed = (
        P("seq", "dp", None),
        P("seq", None),
        P("dp", None),
        P(),
        P(),
        P("dp", None),
        P(),
        P(),
        P(),
        P(),
        P(),
        P("dp", "seq", None),
    )
    return jax.shard_map(
        local,
        mesh=mesh,
        in_specs=placed,
        out_specs=(P("dp", "seq", None), P("dp", "seq", None)),
        check_vma=False,
    )
```

```python
import functools

import jax
import jax.numpy as jnp
import numpy as np
from jax import lax
from jax.experimental import pallas as pl
from jax.experimental.pallas import tpu as pltpu
from jax.sharding import PartitionSpec as P

BLK = 8
PITCH = 32
WIDE = BLK * PITCH
MEL_STEP = 20
MEL_LEAD = 4
MEL_KEEP = 27
FULL = 4
BINS = FULL + 1
BINS_IN = 13
BIN_ORDER = tuple(range(0, BINS_IN, 2)) + tuple(range(1, BINS_IN, 2))
EVENS = (BINS_IN + 1) // 2
RIM = 32
PROJ_PARTS = 4
CONV_ROWS = 256
F32 = jnp.float32
BF16 = jnp.bfloat16
VMEM = pl.BlockSpec(memory_space=pltpu.VMEM)
SMEM = pl.BlockSpec(memory_space=pltpu.SMEM)
HBM = pl.BlockSpec(memory_space=pltpu.HBM)


def iota(shape, dim):
    return lax.broadcasted_iota(jnp.int32, shape, dim)


def one_hot(condition):
    return jnp.where(condition, 1.0, 0.0).astype(BF16)


def dot(left, right):
    return jnp.dot(left, right, preferred_element_type=F32)


def dot_rows(left, right):
    return lax.dot_general(left, right, (((0,), (0,)), ((), ())), preferred_element_type=F32)


def dot_cols(left, right):
    return lax.dot_general(left, right, (((1,), (1,)), ((), ())), preferred_element_type=F32)


def send_kernel(place_ref, frames_ref, dest_ref, proj_ref, out_ref, same_ref, other_ref):
    group = place_ref[0]
    blocks = frames_ref.shape[0]
    span = pl.multiple_of((group // 2) * 128, 128)
    pair = dest_ref[:, pl.ds(span, 128)]
    pair = jnp.where(group % 2 == 1, pltpu.roll(pair, 128 - blocks, 1), pair)
    row = jnp.broadcast_to(pair, (128, 128)) // blocks
    at_row, at_col = iota((128, 128), 0), iota((128, 128), 1)
    column = jnp.sum(jnp.where(at_row == at_col, row, 0), axis=1, keepdims=True)
    same = (row == column) & (at_row < at_col) & (at_row < blocks)
    rank = jnp.sum(jnp.where(same, 1, 0), axis=0, keepdims=True)
    slot = (row[0:1] * 2 + rank)[:, 0:blocks]
    sorted_blocks = dot(one_hot(iota((2 * blocks, blocks), 0) == slot), frames_ref[...])
    out_ref[...] = sorted_blocks.astype(BF16).reshape(out_ref.shape)
    half = same_ref.shape[1]
    left, right = proj_ref[:, 0:half], proj_ref[:, half : 2 * half]
    odd = group % 2 == 1
    same_ref[...] = jnp.where(odd, right, left)
    other_ref[...] = jnp.where(odd, left, right)


def landing_kernel(place_ref, dest_ref, out_ref):
    group = place_ref[0]
    _, groups, blocks = out_ref.shape
    rows = [dest_ref[:, at : at + 128] for at in range(0, groups * blocks, 128)]
    dest = jnp.concatenate(rows, axis=0)
    dest = jnp.concatenate([dest, pltpu.roll(dest, 128 - blocks, 1)], axis=0)[:, 0:blocks]
    at_row, at_col = iota((groups, groups), 0), iota((groups, groups), 1)
    pairs = groups // 2
    order = one_hot(at_row == jnp.where(at_col < pairs, 2 * at_col, 2 * (at_col - pairs) + 1))
    mine = dest // blocks == group
    earlier = one_hot(iota((blocks, blocks), 0) < iota((blocks, blocks), 1))
    rank = dot(one_hot(mine), earlier)
    spot = dest % blocks
    for copy in range(2):
        kept = jnp.where(mine & (rank == float(copy)), spot + 1, 0)
        landing = jnp.sum(kept, axis=1, keepdims=True) - 1
        landing = one_hot(iota((groups, blocks), 1) == landing)
        out_ref[copy] = dot(order, landing).astype(BF16)


def place_kernel(place_ref, arrived_ref, landing_ref, cut_ref, cot_ref, *out_refs):
    group, seat = place_ref[0], place_ref[1]
    window_ref = out_refs[-1]
    blocks = landing_ref.shape[2]
    arrived = arrived_ref[...]
    placed = dot_rows(landing_ref[0], arrived[:, 0, :]) + dot_rows(
        landing_ref[1], arrived[:, 1, :]
    )
    seats = len(out_refs) - 1
    window_ref[...] = dot(placed.astype(BF16), cut_ref[...]).astype(BF16)
    count = cot_ref.shape[0]
    for step in range(seats):
        share = ((seat + step) % seats) ^ (group // 16)
        span = pl.ds(pl.multiple_of(share * WIDE, WIDE), WIDE)
        out_refs[step][0:blocks, :] = window_ref[:, span]
        if step in (1, seats - 1):
            begin = count - 16 if step == 1 else 0
            for piece in range(cot_ref.shape[1] // WIDE):
                columns = slice(piece * WIDE, (piece + 1) * WIDE)
                rows = slice(blocks + 16 * piece, blocks + 16 * piece + 16)
                out_refs[step][rows, :] = cot_ref[begin : begin + 16, columns]


def row_starts(share):
    start_a = jnp.where(share == 0, 2176, jnp.where(share == 2, 128, 0))
    start_b = jnp.where(share == 1, 2304, jnp.where(share == 3, 256, 2432))
    return 128 * share + 128, start_a, start_b


def proj_copy(proj_hbm, proj_ref, sems, part):
    size = proj_hbm.shape[0] // PROJ_PARTS
    return pltpu.make_async_copy(
        proj_hbm.at[pl.ds(part * size, size)],
        proj_ref.at[pl.ds(128 + part * size, size)],
        sems.at[part],
    )


def project(features, share, proj_ref, wait):
    start, start_a, start_b = row_starts(share)
    result = None
    wait(0)
    for index in range(FULL + 2):
        if index < PROJ_PARTS - 1:
            wait(index + 1)
        if index < FULL:
            at, size, column = start + 512 * index, 512, 512 * index
        else:
            at, size = (start_a, 256) if index == FULL else (start_b, 256)
            column = 512 * FULL + 256 * (index - FULL)
        weight = proj_ref[pl.ds(pl.multiple_of(at, 128), size), :]
        part = dot(features(column, size), weight)
        result = part if result is None else result + part
    return result


def zero_rims(proj_ref, rows):
    rim = jnp.zeros((128, proj_ref.shape[1]), BF16)
    proj_ref[0:128, :] = rim
    proj_ref[128 + rows : 256 + rows, :] = rim


def conv_kernel(place_ref, lengths_ref, *refs):
    block_refs, (conv1_ref, conv2_hbm), refs = refs[:4], refs[4:6], refs[6:]
    out_ref, conv2_ref, patch_ref, first_ref, conv2_sems = refs
    group, seat = place_ref[0], place_ref[1]
    share = seat ^ (group // 16)
    taps, channels = conv2_ref.shape[0], conv2_ref.shape[1]
    frames = out_ref.shape[0]
    conv2_copies = [
        pltpu.make_async_copy(conv2_hbm.at[tap], conv2_ref.at[tap], conv2_sems.at[tap])
        for tap in range(taps)
    ]
    for copy in conv2_copies:
        copy.start()
    windows = jnp.concatenate([block_ref[0:64, :] for block_ref in block_refs], axis=0)
    count = windows.shape[0]
    frame = (seat * 128 + iota((frames, count), 0)) % (2 * count)
    block = iota((frames, count), 1)
    block = ((seat + 4 - block // 64) % 4) * 64 + block % 64
    own_block = frame // 2
    second = lengths_ref[0]
    third = second + lengths_ref[1]
    begins = (own_block == 0) | (own_block == second) | (own_block == third)
    odd = frame % 2 == 1
    here = own_block == block
    before = (own_block - 1 == block) & jnp.logical_not(begins)
    here_odd = dot(one_hot(odd & here), windows)
    here_even = dot(one_hot(jnp.logical_not(odd) & here), windows)
    prev_even = dot(one_hot(jnp.logical_not(odd) & before), windows)
    lane = iota((frames, WIDE), 1)
    patches = pltpu.roll(here_odd, WIDE - PITCH, 1) + pltpu.roll(
        jnp.where(lane < 5 * PITCH, here_even, prev_even), 3 * PITCH, 1
    )
    for index, mel_bin in enumerate(BIN_ORDER):
        moved = patches if mel_bin == 0 else pltpu.roll(patches, WIDE - 2 * mel_bin, 1)
        patch_ref[index * frames : (index + 1) * frames, :] = moved.astype(BF16)
    tap_lane, tap_at = iota((WIDE, 16), 0), iota((WIDE, 16), 1)
    all_rows = BINS_IN * frames
    for row_tap in range(3):
        spread = (2 * row_tap + tap_at // 3) * PITCH + tap_at % 3
        weight = dot(one_hot((tap_lane == spread) & (tap_at < 9)), conv1_ref[...]).astype(BF16)
        for start in range(0, all_rows, 512):
            stop = min(start + 512, all_rows)
            response = dot(patch_ref[start:stop, :], weight)
            first_ref[row_tap, start:stop, :] = jnp.maximum(response, 0.0).astype(BF16)
    whole_rows = (1, EVENS + 1, 2)
    half_rows = (0, EVENS, 1)
    bin_a = jnp.where(share == 0, 5, 0)
    bin_b = jnp.where(share == 3, 0, 5)
    side_a = jnp.where((share == 1) | (share == 2), 1, 0)
    side_b = jnp.where((share == 0) | (share == 3), 1, 0)
    half = channels // 2
    for copy in conv2_copies:
        copy.wait()
    for begin in range(0, frames, CONV_ROWS):
        for part in range(FULL):
            total = None
            for tap in range(taps):
                at = (whole_rows[tap % 3] + part) * frames + begin
                product = dot(first_ref[tap // 3, at : at + CONV_ROWS, :], conv2_ref[tap])
                total = product if total is None else total + product
            columns = slice(part * channels, (part + 1) * channels)
            out_ref[begin : begin + CONV_ROWS, columns] = jnp.maximum(total, 0.0).astype(BF16)
        for index, (mel_bin, side) in enumerate(((bin_a, side_a), (bin_b, side_b))):
            columns = pl.ds(pl.multiple_of(side * half, 128), half)
            total = None
            for tap in range(taps):
                at = (half_rows[tap % 3] + mel_bin) * frames + begin
                rows = pl.ds(pl.multiple_of(at, 128), CONV_ROWS)
                product = dot(first_ref[tap // 3, rows, :], conv2_ref[tap, :, columns])
                total = product if total is None else total + product
            first = FULL * channels + index * half
            columns = slice(first, first + half)
            out_ref[begin : begin + CONV_ROWS, columns] = jnp.maximum(total, 0.0).astype(BF16)


def conv_features(place, lengths, blocks, conv1_weight, conv2_weight, frames):
    taps, channels, _ = conv2_weight.shape
    return pl.pallas_call(
        conv_kernel,
        out_shape=jax.ShapeDtypeStruct((frames, BINS * channels), BF16),
        in_specs=[SMEM] * 2 + [VMEM] * 5 + [HBM],
        out_specs=VMEM,
        scratch_shapes=[
            pltpu.VMEM(conv2_weight.shape, BF16),
            pltpu.VMEM((BINS_IN * frames, WIDE), BF16),
            pltpu.VMEM((3, BINS_IN * frames, channels), BF16),
            pltpu.SemaphoreType.DMA((taps,)),
        ],
        compiler_params=pltpu.CompilerParams(vmem_limit_bytes=48 * 1024 * 1024),
        name="convolutions",
    )(place, lengths, *blocks, conv1_weight, conv2_weight)


def proj_kernel(place_ref, features_ref, proj_hbm, *refs):
    out_refs, (result_ref, proj_ref, sems) = refs[:-3], refs[-3:]
    group, seat = place_ref[0], place_ref[1]
    for part in range(PROJ_PARTS):
        proj_copy(proj_hbm, proj_ref, sems, part).start()
    zero_rims(proj_ref, proj_hbm.shape[0])

    def features(column, size):
        return features_ref[:, column : column + size]

    def wait(part):
        proj_copy(proj_hbm, proj_ref, sems, part).wait()

    result = project(features, seat ^ (group // 16), proj_ref, wait)
    result_ref[...] = result.astype(BF16)
    count = result_ref.shape[0]
    own = count // len(out_refs)
    for step, out_ref in enumerate(out_refs):
        for at in range(0, own + 2 * RIM, RIM):
            source = (step * own - RIM + at) % count
            out_ref[at : at + RIM, :] = result_ref[source : source + RIM, :]


def projected_parts(place, features, proj, seats):
    rows, half = proj.shape
    frames = features.shape[0]
    shape = jax.ShapeDtypeStruct((frames // seats + 2 * RIM, half), BF16)
    return pl.pallas_call(
        proj_kernel,
        out_shape=[shape] * seats,
        in_specs=[SMEM, VMEM, HBM],
        out_specs=[VMEM] * seats,
        scratch_shapes=[
            pltpu.VMEM((frames, half), BF16),
            pltpu.VMEM((rows + 256, half), BF16),
            pltpu.SemaphoreType.DMA((PROJ_PARTS,)),
        ],
        compiler_params=pltpu.CompilerParams(vmem_limit_bytes=40 * 1024 * 1024),
        name="projection",
    )(place, features, proj)


def layer_norm(values):
    average = jnp.mean(values, axis=-1, keepdims=True)
    centered = values - average
    inverse = lax.rsqrt(jnp.mean(centered * centered, axis=-1, keepdims=True) + 1e-05)
    return centered * inverse, inverse


def norm_back(d_normed, normed, inverse):
    return (
        d_normed
        - jnp.mean(d_normed, axis=-1, keepdims=True)
        - normed * jnp.mean(d_normed * normed, axis=-1, keepdims=True)
    ) * inverse


def depthwise(source, seg_ref, taps_ref, moved_ref, out_ref, base, seg_base, count, reverse):
    kernel, width = taps_ref.shape
    half = (kernel - 1) // 2
    length = source.shape[0]
    for residue in range(8):
        for index in range(width // 128):
            lanes = slice(index * 128, (index + 1) * 128)
            column = source[:, lanes]
            if residue:
                column = pltpu.roll(column, length - residue, 0)
            moved_ref[residue, 0:length, lanes] = column
    step = 32
    for begin in range(0, count, step):
        mine = seg_ref[0, seg_base + begin : seg_base + begin + step, :]
        running = [jnp.zeros((step, 128), F32) for _ in range(width // 128)]
        for offset in range(kernel):
            shift = half - offset if reverse else offset - half
            residue = shift % 8
            other = seg_base + begin + shift - residue
            same = seg_ref[residue, other : other + step, :] == mine
            at = base + begin + shift - residue
            for index in range(width // 128):
                lanes = slice(index * 128, (index + 1) * 128)
                window = jnp.where(same, moved_ref[residue, at : at + step, lanes], 0.0)
                running[index] = running[index] + window * taps_ref[offset : offset + 1, lanes]
        for index in range(width // 128):
            out_ref[begin : begin + step, index * 128 : (index + 1) * 128] = running[index]


def module_kernel(
    place_ref,
    lengths_ref,
    same_0_ref,
    same_1_ref,
    same_2_ref,
    same_3_ref,
    other_0_ref,
    other_1_ref,
    other_2_ref,
    other_3_ref,
    cot_low_ref,
    cot_ref,
    cot_high_ref,
    gain_in_ref,
    point_in_ref,
    taps_ref,
    gain_mid_ref,
    point_out_ref,
    encoded_ref,
    grad_ref,
    glu_ref,
    seg_ref,
    mixed_ref,
    back_ref,
):
    own, width = cot_ref.shape
    total = own + 2 * RIM
    inner = own + RIM
    skip = RIM // 2
    same = same_0_ref[...].astype(F32) + same_1_ref[...].astype(F32)
    same = same + same_2_ref[...].astype(F32) + same_3_ref[...].astype(F32)
    other = other_0_ref[...].astype(F32) + other_1_ref[...].astype(F32)
    other = other + other_2_ref[...].astype(F32) + other_3_ref[...].astype(F32)
    odd = place_ref[0] % 2 == 1
    halves = [jnp.where(odd, other, same), jnp.where(odd, same, other)]
    encoder = jnp.concatenate(halves, axis=1).astype(BF16).astype(F32)
    normed_in, inv_in = layer_norm(encoder)
    ln_in = (normed_in * gain_in_ref[...]).astype(BF16)
    left = dot(ln_in, point_in_ref[:, 0:width])
    gate = jax.nn.sigmoid(dot(ln_in, point_in_ref[:, width : 2 * width]))
    glu_out = (left * gate).astype(BF16).astype(F32)
    frame = place_ref[1] * own - RIM + iota((total, 128), 0)
    block = (frame + 4 * RIM) // 2 - 2 * RIM
    second = lengths_ref[0]
    third = second + lengths_ref[1]
    ends = third + lengths_ref[2]
    seg = (
        jnp.where(block >= 0, 1, 0)
        + jnp.where(block >= second, 1, 0)
        + jnp.where(block >= third, 1, 0)
        + jnp.where(block >= ends, 1, 0)
    )
    for residue in range(8):
        seg_ref[residue] = pltpu.roll(seg, total - residue, 0) if residue else seg
    depthwise(glu_out, seg_ref, taps_ref, glu_ref, mixed_ref, skip, skip, inner, False)
    normed_mid, inv_mid = layer_norm(mixed_ref[...])
    scaled = normed_mid * gain_mid_ref[...]
    logistic = jax.nn.sigmoid(scaled)
    slope = logistic * (1.0 + scaled * (1.0 - logistic))
    low = RIM - skip
    hidden = (scaled * logistic)[low : low + own].astype(BF16)
    encoded = encoder[RIM : RIM + own] + dot(hidden, point_out_ref[...])
    encoded_ref[...] = encoded.astype(BF16)
    low_edge, high_edge = [
        jnp.concatenate([ref[64 + 16 * piece : 80 + 16 * piece, :] for piece in range(3)], axis=1)
        for ref in (cot_low_ref, cot_high_ref)
    ]
    cotangent = jnp.concatenate([low_edge, cot_ref[...], high_edge], axis=0)
    d_hidden = dot_cols(cotangent, point_out_ref[...])
    d_mixed = norm_back(d_hidden * slope * gain_mid_ref[...], normed_mid, inv_mid)
    d_mixed = d_mixed.astype(BF16).astype(F32)
    depthwise(d_mixed, seg_ref, taps_ref, glu_ref, back_ref, low, RIM, own, True)
    d_glu = back_ref[...]
    own_gate = gate[RIM : RIM + own]
    d_left = d_glu * own_gate
    d_right = d_left * left[RIM : RIM + own] * (1.0 - own_gate)
    d_normed = dot_cols(d_left.astype(BF16), point_in_ref[:, 0:width])
    d_normed = d_normed + dot_cols(d_right.astype(BF16), point_in_ref[:, width : 2 * width])
    own_normed = normed_in[RIM : RIM + own]
    back = norm_back(d_normed * gain_in_ref[...], own_normed, inv_in[RIM : RIM + own])
    grad_ref[...] = (cot_ref[...].astype(F32) + back).astype(BF16)


def conv_module(place, lengths, parts, cotangents, gain_in, point_in, taps, gain_mid, point_out):
    own, width = cotangents[1].shape
    inner = own + RIM
    shape = jax.ShapeDtypeStruct((own, width), BF16)
    return pl.pallas_call(
        module_kernel,
        out_shape=(shape, shape),
        in_specs=[SMEM, SMEM] + [VMEM] * 16,
        out_specs=(VMEM, VMEM),
        scratch_shapes=[
            pltpu.VMEM((8, own + 2 * RIM, width), F32),
            pltpu.VMEM((8, own + 2 * RIM, 128), jnp.int32),
            pltpu.VMEM((inner, width), F32),
            pltpu.VMEM((own, width), F32),
        ],
        compiler_params=pltpu.CompilerParams(vmem_limit_bytes=48 * 1024 * 1024),
        name="conv_module",
    )(place, lengths, *parts, *cotangents, gain_in[None], point_in, taps, gain_mid[None], point_out)
def send(place, frames, block_dest, proj_weight):
    blocks, width = frames.shape
    rows, columns = proj_weight.shape
    shape = jax.ShapeDtypeStruct((rows, columns // 2), BF16)
    return pl.pallas_call(
        send_kernel,
        out_shape=(jax.ShapeDtypeStruct((blocks, 2, width), BF16), shape, shape),
        in_specs=[SMEM, VMEM, VMEM, VMEM],
        out_specs=(VMEM, VMEM, VMEM),
        name="send",
    )(place, frames, block_dest, proj_weight)


def landing_slots(place, block_dest, groups, blocks):
    return pl.pallas_call(
        landing_kernel,
        out_shape=jax.ShapeDtypeStruct((2, groups, blocks), BF16),
        in_specs=[SMEM, VMEM],
        out_specs=VMEM,
        name="landing",
    )(place, block_dest)


def cut_matrix(seats, width):
    mel_bins = width // BLK
    share, frame, mel = np.meshgrid(
        np.arange(seats), np.arange(BLK), np.arange(PITCH), indexing="ij"
    )
    source = MEL_STEP * share - MEL_LEAD + mel
    fits = (mel < MEL_KEEP) & (source >= 0) & (source < mel_bins)
    source = np.where(fits, frame * mel_bins + source, -1).reshape(-1)
    return jnp.asarray(np.arange(width)[:, None] == source[None, :], BF16)


def place_blocks(place, arrived, landing, cotangent, seats):
    blocks = landing.shape[2]
    rim_rows = 16 * cotangent.shape[1] // WIDE
    rows = [blocks + (rim_rows if step in (1, seats - 1) else 0) for step in range(seats)]
    return pl.pallas_call(
        place_kernel,
        out_shape=[jax.ShapeDtypeStruct((count, WIDE), BF16) for count in rows],
        in_specs=[SMEM, VMEM, VMEM, VMEM, VMEM],
        out_specs=[VMEM] * seats,
        scratch_shapes=[pltpu.VMEM((blocks, seats * WIDE), BF16)],
        name="place",
    )(place, arrived, landing, cut_matrix(seats, arrived.shape[2]), cotangent)


def share_routes(groups, seats, flip):
    cluster = groups // seats
    routes = []
    for group in range(groups):
        for seat in range(seats):
            target = ((group // cluster) ^ seat) * cluster + (group % cluster ^ flip)
            routes.append((group * seats + seat, target * seats + seat))
    return routes


def gather_share(pair, groups, cluster):
    members = [
        [begin + core + 2 * index for index in range(cluster // 2)]
        for begin in range(0, groups, cluster)
        for core in range(2)
    ]
    rows, half = pair.shape
    copies = jnp.broadcast_to(pair[None], (cluster // 2, rows, half))
    same = lax.all_to_all(
        copies, "dp", split_axis=0, concat_axis=0, tiled=True, axis_index_groups=members
    ).reshape(-1, half)
    return same


def local(
    loader_frames,
    block_dest,
    utt_lengths,
    conv1_weight,
    conv2_weight,
    proj_weight,
    gain_in,
    point_in,
    taps,
    gain_mid,
    point_out,
    grad_encoded,
):
    groups, seats = lax.axis_size("dp"), lax.axis_size("seq")
    group, seat = lax.axis_index("dp"), lax.axis_index("seq")
    place = jnp.stack([group, seat]).astype(jnp.int32)
    lengths = utt_lengths[0]
    frames = loader_frames[0]
    blocks = frames.shape[0]
    cotangent = grad_encoded[0]
    own, width = cotangent.shape
    channels = conv2_weight.shape[1]
    rows = proj_weight.shape[0]
    cluster = groups // seats
    half = width // 2
    core = group % 2
    outgoing, same, other = send(place, frames, block_dest, proj_weight)
    same = lax.ppermute(same, ("dp", "seq"), share_routes(groups, seats, 0))
    other = lax.ppermute(other, ("dp", "seq"), share_routes(groups, seats, 1))
    arrived = lax.all_to_all(outgoing, "dp", split_axis=0, concat_axis=0, tiled=True)
    landing = landing_slots(place, block_dest, groups, blocks)
    windows = place_blocks(place, arrived, landing, cotangent, seats)
    pair = jnp.where(
        core == 0,
        jnp.concatenate([same, other], axis=0),
        jnp.concatenate([other, same], axis=0),
    )

    def ring(step):
        return [(index, (index + step) % seats) for index in range(seats)]

    windows = [windows[0]] + [
        lax.ppermute(windows[step], "seq", ring(step)) for step in range(1, seats)
    ]
    pair, *windows = lax.optimization_barrier((pair, *windows))
    same = gather_share(pair, groups, cluster)
    conv1 = jnp.pad(conv1_weight, ((0, 16 - conv1_weight.shape[0]), (0, 0)))
    features = conv_features(place, lengths, windows, conv1, conv2_weight, seats * own)
    features, same = lax.optimization_barrier((features, same))
    other = lax.ppermute(same, "dp", [(index, index ^ 1) for index in range(groups)])
    parts = []
    for proj in (same, other):
        sums = projected_parts(place, features, proj, seats)
        parts += [sums[0]] + [
            lax.ppermute(sums[step], "seq", ring(step)) for step in range(1, seats)
        ]
    encoded, grad_input = conv_module(
        place,
        lengths,
        parts,
        (windows[1], cotangent, windows[3]),
        gain_in,
        point_in,
        taps,
        gain_mid,
        point_out,
    )
    return encoded[None], grad_input[None]


def solution(mesh):
    placed = (
        P("seq", "dp", None),
        P("seq", None),
        P("dp", None),
        P(),
        P(),
        P("dp", None),
        P(),
        P(),
        P(),
        P(),
        P(),
        P("dp", "seq", None),
    )
    return jax.shard_map(
        local,
        mesh=mesh,
        in_specs=placed,
        out_specs=(P("dp", "seq", None), P("dp", "seq", None)),
        check_vma=False,
    )
```

```python
import functools

import jax
import jax.numpy as jnp
import numpy as np
from jax import lax
from jax.experimental import pallas as pl
from jax.experimental.pallas import tpu as pltpu
from jax.sharding import PartitionSpec as P

BLK = 8
PITCH = 32
WIDE = BLK * PITCH
MEL_STEP = 20
MEL_LEAD = 4
MEL_KEEP = 27
FULL = 4
BINS = FULL + 1
BINS_IN = 13
BIN_ORDER = tuple(range(0, BINS_IN, 2)) + tuple(range(1, BINS_IN, 2))
EVENS = (BINS_IN + 1) // 2
RIM = 32
PROJ_PARTS = 4
CONV_ROWS = 256
F32 = jnp.float32
BF16 = jnp.bfloat16
VMEM = pl.BlockSpec(memory_space=pltpu.VMEM)
SMEM = pl.BlockSpec(memory_space=pltpu.SMEM)
HBM = pl.BlockSpec(memory_space=pltpu.HBM)


def iota(shape, dim):
    return lax.broadcasted_iota(jnp.int32, shape, dim)


def one_hot(condition):
    return jnp.where(condition, 1.0, 0.0).astype(BF16)


def dot(left, right):
    return jnp.dot(left, right, preferred_element_type=F32)


def dot_rows(left, right):
    return lax.dot_general(left, right, (((0,), (0,)), ((), ())), preferred_element_type=F32)


def dot_cols(left, right):
    return lax.dot_general(left, right, (((1,), (1,)), ((), ())), preferred_element_type=F32)


def send_kernel(place_ref, frames_ref, dest_ref, proj_ref, out_ref, same_ref, other_ref):
    group = place_ref[0]
    blocks = frames_ref.shape[0]
    span = pl.multiple_of((group // 2) * 128, 128)
    pair = dest_ref[:, pl.ds(span, 128)]
    pair = jnp.where(group % 2 == 1, pltpu.roll(pair, 128 - blocks, 1), pair)
    row = jnp.broadcast_to(pair, (128, 128)) // blocks
    at_row, at_col = iota((128, 128), 0), iota((128, 128), 1)
    column = jnp.sum(jnp.where(at_row == at_col, row, 0), axis=1, keepdims=True)
    same = (row == column) & (at_row < at_col) & (at_row < blocks)
    rank = jnp.sum(jnp.where(same, 1, 0), axis=0, keepdims=True)
    slot = (row[0:1] * 2 + rank)[:, 0:blocks]
    sorted_blocks = dot(one_hot(iota((2 * blocks, blocks), 0) == slot), frames_ref[...])
    out_ref[...] = sorted_blocks.astype(BF16).reshape(out_ref.shape)
    half = same_ref.shape[1]
    left, right = proj_ref[:, 0:half], proj_ref[:, half : 2 * half]
    odd = group % 2 == 1
    same_ref[...] = jnp.where(odd, right, left)
    other_ref[...] = jnp.where(odd, left, right)


def landing_kernel(place_ref, dest_ref, out_ref):
    group = place_ref[0]
    _, groups, blocks = out_ref.shape
    rows = [dest_ref[:, at : at + 128] for at in range(0, groups * blocks, 128)]
    dest = jnp.concatenate(rows, axis=0)
    dest = jnp.concatenate([dest, pltpu.roll(dest, 128 - blocks, 1)], axis=0)[:, 0:blocks]
    at_row, at_col = iota((groups, groups), 0), iota((groups, groups), 1)
    pairs = groups // 2
    order = one_hot(at_row == jnp.where(at_col < pairs, 2 * at_col, 2 * (at_col - pairs) + 1))
    mine = dest // blocks == group
    earlier = one_hot(iota((blocks, blocks), 0) < iota((blocks, blocks), 1))
    rank = dot(one_hot(mine), earlier)
    spot = dest % blocks
    for copy in range(2):
        kept = jnp.where(mine & (rank == float(copy)), spot + 1, 0)
        landing = jnp.sum(kept, axis=1, keepdims=True) - 1
        landing = one_hot(iota((groups, blocks), 1) == landing)
        out_ref[copy] = dot(order, landing).astype(BF16)


def place_kernel(place_ref, arrived_ref, landing_ref, cut_ref, cot_ref, *out_refs):
    group, seat = place_ref[0], place_ref[1]
    window_ref = out_refs[-1]
    blocks = landing_ref.shape[2]
    arrived = arrived_ref[...]
    placed = dot_rows(landing_ref[0], arrived[:, 0, :]) + dot_rows(
        landing_ref[1], arrived[:, 1, :]
    )
    seats = len(out_refs) - 1
    window_ref[...] = dot(placed.astype(BF16), cut_ref[...]).astype(BF16)
    count = cot_ref.shape[0]
    for step in range(seats):
        share = ((seat + step) % seats) ^ (group // 16)
        span = pl.ds(pl.multiple_of(share * WIDE, WIDE), WIDE)
        out_refs[step][0:blocks, :] = window_ref[:, span]
        if step in (1, seats - 1):
            begin = count - 16 if step == 1 else 0
            for piece in range(cot_ref.shape[1] // WIDE):
                columns = slice(piece * WIDE, (piece + 1) * WIDE)
                rows = slice(blocks + 16 * piece, blocks + 16 * piece + 16)
                out_refs[step][rows, :] = cot_ref[begin : begin + 16, columns]


def row_starts(share):
    start_a = jnp.where(share == 0, 2176, jnp.where(share == 2, 128, 0))
    start_b = jnp.where(share == 1, 2304, jnp.where(share == 3, 256, 2432))
    return 128 * share + 128, start_a, start_b


def proj_copy(proj_hbm, proj_ref, sems, part):
    size = proj_hbm.shape[0] // PROJ_PARTS
    return pltpu.make_async_copy(
        proj_hbm.at[pl.ds(part * size, size)],
        proj_ref.at[pl.ds(128 + part * size, size)],
        sems.at[part],
    )


def project(features, share, proj_ref, wait):
    start, start_a, start_b = row_starts(share)
    result = None
    wait(0)
    for index in range(FULL + 2):
        if index < PROJ_PARTS - 1:
            wait(index + 1)
        if index < FULL:
            at, size, column = start + 512 * index, 512, 512 * index
        else:
            at, size = (start_a, 256) if index == FULL else (start_b, 256)
            column = 512 * FULL + 256 * (index - FULL)
        weight = proj_ref[pl.ds(pl.multiple_of(at, 128), size), :]
        part = dot(features(column, size), weight)
        result = part if result is None else result + part
    return result


def zero_rims(proj_ref, rows):
    rim = jnp.zeros((128, proj_ref.shape[1]), BF16)
    proj_ref[0:128, :] = rim
    proj_ref[128 + rows : 256 + rows, :] = rim


def conv_kernel(place_ref, lengths_ref, *refs):
    block_refs, (conv1_ref, conv2_hbm), refs = refs[:4], refs[4:6], refs[6:]
    out_ref, conv2_ref, patch_ref, first_ref, conv2_sems = refs
    group, seat = place_ref[0], place_ref[1]
    share = seat ^ (group // 16)
    taps, channels = conv2_ref.shape[0], conv2_ref.shape[1]
    frames = out_ref.shape[0]
    conv2_copies = [
        pltpu.make_async_copy(conv2_hbm.at[tap], conv2_ref.at[tap], conv2_sems.at[tap])
        for tap in range(taps)
    ]
    for copy in conv2_copies:
        copy.start()
    windows = jnp.concatenate([block_ref[0:64, :] for block_ref in block_refs], axis=0)
    count = windows.shape[0]
    frame = (seat * 128 + iota((frames, count), 0)) % (2 * count)
    block = iota((frames, count), 1)
    block = ((seat + 4 - block // 64) % 4) * 64 + block % 64
    own_block = frame // 2
    second = lengths_ref[0]
    third = second + lengths_ref[1]
    begins = (own_block == 0) | (own_block == second) | (own_block == third)
    odd = frame % 2 == 1
    here = own_block == block
    before = (own_block - 1 == block) & jnp.logical_not(begins)
    here_odd = dot(one_hot(odd & here), windows)
    here_even = dot(one_hot(jnp.logical_not(odd) & here), windows)
    prev_even = dot(one_hot(jnp.logical_not(odd) & before), windows)
    lane = iota((frames, WIDE), 1)
    patches = pltpu.roll(here_odd, WIDE - PITCH, 1) + pltpu.roll(
        jnp.where(lane < 5 * PITCH, here_even, prev_even), 3 * PITCH, 1
    )
    for index, mel_bin in enumerate(BIN_ORDER):
        moved = patches if mel_bin == 0 else pltpu.roll(patches, WIDE - 2 * mel_bin, 1)
        patch_ref[index * frames : (index + 1) * frames, :] = moved.astype(BF16)
    tap_lane, tap_at = iota((WIDE, 16), 0), iota((WIDE, 16), 1)
    all_rows = BINS_IN * frames
    for row_tap in range(3):
        spread = (2 * row_tap + tap_at // 3) * PITCH + tap_at % 3
        weight = dot(one_hot((tap_lane == spread) & (tap_at < 9)), conv1_ref[...]).astype(BF16)
        for start in range(0, all_rows, 512):
            stop = min(start + 512, all_rows)
            response = dot(patch_ref[start:stop, :], weight)
            first_ref[row_tap, start:stop, :] = jnp.maximum(response, 0.0).astype(BF16)
    whole_rows = (1, EVENS + 1, 2)
    half_rows = (0, EVENS, 1)
    bin_a = jnp.where(share == 0, 5, 0)
    bin_b = jnp.where(share == 3, 0, 5)
    side_a = jnp.where((share == 1) | (share == 2), 1, 0)
    side_b = jnp.where((share == 0) | (share == 3), 1, 0)
    half = channels // 2
    for copy in conv2_copies:
        copy.wait()
    for begin in range(0, frames, CONV_ROWS):
        for part in range(FULL):
            total = None
            for tap in range(taps):
                at = (whole_rows[tap % 3] + part) * frames + begin
                product = dot(first_ref[tap // 3, at : at + CONV_ROWS, :], conv2_ref[tap])
                total = product if total is None else total + product
            columns = slice(part * channels, (part + 1) * channels)
            out_ref[begin : begin + CONV_ROWS, columns] = jnp.maximum(total, 0.0).astype(BF16)
        for index, (mel_bin, side) in enumerate(((bin_a, side_a), (bin_b, side_b))):
            columns = pl.ds(pl.multiple_of(side * half, 128), half)
            total = None
            for tap in range(taps):
                at = (half_rows[tap % 3] + mel_bin) * frames + begin
                rows = pl.ds(pl.multiple_of(at, 128), CONV_ROWS)
                product = dot(first_ref[tap // 3, rows, :], conv2_ref[tap, :, columns])
                total = product if total is None else total + product
            first = FULL * channels + index * half
            columns = slice(first, first + half)
            out_ref[begin : begin + CONV_ROWS, columns] = jnp.maximum(total, 0.0).astype(BF16)


def conv_features(place, lengths, blocks, conv1_weight, conv2_weight, frames):
    taps, channels, _ = conv2_weight.shape
    return pl.pallas_call(
        conv_kernel,
        out_shape=jax.ShapeDtypeStruct((frames, BINS * channels), BF16),
        in_specs=[SMEM] * 2 + [VMEM] * 5 + [HBM],
        out_specs=VMEM,
        scratch_shapes=[
            pltpu.VMEM(conv2_weight.shape, BF16),
            pltpu.VMEM((BINS_IN * frames, WIDE), BF16),
            pltpu.VMEM((3, BINS_IN * frames, channels), BF16),
            pltpu.SemaphoreType.DMA((taps,)),
        ],
        compiler_params=pltpu.CompilerParams(vmem_limit_bytes=48 * 1024 * 1024),
        name="convolutions",
    )(place, lengths, *blocks, conv1_weight, conv2_weight)


def proj_kernel(place_ref, features_hbm, proj_hbm, *refs):
    out_refs, refs = refs[:-5], refs[-5:]
    result_ref, proj_ref, sems, features_ref, feature_sems = refs
    group, seat = place_ref[0], place_ref[1]
    blocks = feature_sems.shape[0]
    size = features_ref.shape[1] // blocks

    def feature_copy(block):
        columns = pl.ds(block * size, size)
        return pltpu.make_async_copy(
            features_hbm.at[:, columns], features_ref.at[:, columns], feature_sems.at[block]
        )

    for part in range(blocks):
        if part < PROJ_PARTS:
            proj_copy(proj_hbm, proj_ref, sems, part).start()
        feature_copy(part).start()
    zero_rims(proj_ref, proj_hbm.shape[0])

    def features(column, count):
        if column % size == 0:
            feature_copy(column // size).wait()
        return features_ref[:, column : column + count]

    def wait(part):
        proj_copy(proj_hbm, proj_ref, sems, part).wait()

    result = project(features, seat ^ (group // 16), proj_ref, wait)
    result_ref[...] = result.astype(BF16)
    count = result_ref.shape[0]
    own = count // len(out_refs)
    for step, out_ref in enumerate(out_refs):
        for at in range(0, own + 2 * RIM, RIM):
            source = (step * own - RIM + at) % count
            out_ref[at : at + RIM, :] = result_ref[source : source + RIM, :]


def projected_parts(place, features, proj, seats):
    rows, half = proj.shape
    frames = features.shape[0]
    shape = jax.ShapeDtypeStruct((frames // seats + 2 * RIM, half), BF16)
    return pl.pallas_call(
        proj_kernel,
        out_shape=[shape] * seats,
        in_specs=[SMEM, HBM, HBM],
        out_specs=[VMEM] * seats,
        scratch_shapes=[
            pltpu.VMEM((frames, half), BF16),
            pltpu.VMEM((rows + 256, half), BF16),
            pltpu.SemaphoreType.DMA((PROJ_PARTS,)),
            pltpu.VMEM(features.shape, BF16),
            pltpu.SemaphoreType.DMA((BINS,)),
        ],
        compiler_params=pltpu.CompilerParams(vmem_limit_bytes=40 * 1024 * 1024),
        name="projection",
    )(place, features, proj)


def layer_norm(values):
    average = jnp.mean(values, axis=-1, keepdims=True)
    centered = values - average
    inverse = lax.rsqrt(jnp.mean(centered * centered, axis=-1, keepdims=True) + 1e-05)
    return centered * inverse, inverse


def norm_back(d_normed, normed, inverse):
    return (
        d_normed
        - jnp.mean(d_normed, axis=-1, keepdims=True)
        - normed * jnp.mean(d_normed * normed, axis=-1, keepdims=True)
    ) * inverse


def depthwise(source, seg_ref, taps_ref, moved_ref, out_ref, base, seg_base, count, reverse):
    kernel, width = taps_ref.shape
    half = (kernel - 1) // 2
    length = source.shape[0]
    for residue in range(8):
        for index in range(width // 128):
            lanes = slice(index * 128, (index + 1) * 128)
            column = source[:, lanes]
            if residue:
                column = pltpu.roll(column, length - residue, 0)
            moved_ref[residue, 0:length, lanes] = column
    step = 32
    for begin in range(0, count, step):
        mine = seg_ref[0, seg_base + begin : seg_base + begin + step, :]
        running = [jnp.zeros((step, 128), F32) for _ in range(width // 128)]
        for offset in range(kernel):
            shift = half - offset if reverse else offset - half
            residue = shift % 8
            other = seg_base + begin + shift - residue
            same = seg_ref[residue, other : other + step, :] == mine
            at = base + begin + shift - residue
            for index in range(width // 128):
                lanes = slice(index * 128, (index + 1) * 128)
                window = jnp.where(same, moved_ref[residue, at : at + step, lanes], 0.0)
                running[index] = running[index] + window * taps_ref[offset : offset + 1, lanes]
        for index in range(width // 128):
            out_ref[begin : begin + step, index * 128 : (index + 1) * 128] = running[index]


def module_kernel(
    place_ref,
    lengths_ref,
    same_0_ref,
    same_1_ref,
    same_2_ref,
    same_3_ref,
    other_0_ref,
    other_1_ref,
    other_2_ref,
    other_3_ref,
    cot_low_ref,
    cot_ref,
    cot_high_ref,
    gain_in_ref,
    point_in_hbm,
    taps_ref,
    gain_mid_ref,
    point_out_hbm,
    encoded_ref,
    grad_ref,
    glu_ref,
    seg_ref,
    mixed_ref,
    back_ref,
    point_in_ref,
    point_out_ref,
    sems,
):
    point_in_copy = pltpu.make_async_copy(point_in_hbm, point_in_ref, sems.at[0])
    point_out_copy = pltpu.make_async_copy(point_out_hbm, point_out_ref, sems.at[1])
    point_in_copy.start()
    point_out_copy.start()
    own, width = cot_ref.shape
    total = own + 2 * RIM
    inner = own + RIM
    skip = RIM // 2
    same = same_0_ref[...].astype(F32) + same_1_ref[...].astype(F32)
    same = same + same_2_ref[...].astype(F32) + same_3_ref[...].astype(F32)
    other = other_0_ref[...].astype(F32) + other_1_ref[...].astype(F32)
    other = other + other_2_ref[...].astype(F32) + other_3_ref[...].astype(F32)
    odd = place_ref[0] % 2 == 1
    halves = [jnp.where(odd, other, same), jnp.where(odd, same, other)]
    encoder = jnp.concatenate(halves, axis=1).astype(BF16).astype(F32)
    normed_in, inv_in = layer_norm(encoder)
    ln_in = (normed_in * gain_in_ref[...]).astype(BF16)
    point_in_copy.wait()
    left = dot(ln_in, point_in_ref[:, 0:width])
    gate = jax.nn.sigmoid(dot(ln_in, point_in_ref[:, width : 2 * width]))
    glu_out = (left * gate).astype(BF16).astype(F32)
    frame = place_ref[1] * own - RIM + iota((total, 128), 0)
    block = (frame + 4 * RIM) // 2 - 2 * RIM
    second = lengths_ref[0]
    third = second + lengths_ref[1]
    ends = third + lengths_ref[2]
    seg = (
        jnp.where(block >= 0, 1, 0)
        + jnp.where(block >= second, 1, 0)
        + jnp.where(block >= third, 1, 0)
        + jnp.where(block >= ends, 1, 0)
    )
    for residue in range(8):
        seg_ref[residue] = pltpu.roll(seg, total - residue, 0) if residue else seg
    depthwise(glu_out, seg_ref, taps_ref, glu_ref, mixed_ref, skip, skip, inner, False)
    normed_mid, inv_mid = layer_norm(mixed_ref[...])
    scaled = normed_mid * gain_mid_ref[...]
    logistic = jax.nn.sigmoid(scaled)
    slope = logistic * (1.0 + scaled * (1.0 - logistic))
    low = RIM - skip
    point_out_copy.wait()
    hidden = (scaled * logistic)[low : low + own].astype(BF16)
    encoded = encoder[RIM : RIM + own] + dot(hidden, point_out_ref[...])
    encoded_ref[...] = encoded.astype(BF16)
    low_edge, high_edge = [
        jnp.concatenate([ref[64 + 16 * piece : 80 + 16 * piece, :] for piece in range(3)], axis=1)
        for ref in (cot_low_ref, cot_high_ref)
    ]
    cotangent = jnp.concatenate([low_edge, cot_ref[...], high_edge], axis=0)
    d_hidden = dot_cols(cotangent, point_out_ref[...])
    d_mixed = norm_back(d_hidden * slope * gain_mid_ref[...], normed_mid, inv_mid)
    d_mixed = d_mixed.astype(BF16).astype(F32)
    depthwise(d_mixed, seg_ref, taps_ref, glu_ref, back_ref, low, RIM, own, True)
    d_glu = back_ref[...]
    own_gate = gate[RIM : RIM + own]
    d_left = d_glu * own_gate
    d_right = d_left * left[RIM : RIM + own] * (1.0 - own_gate)
    d_normed = dot_cols(d_left.astype(BF16), point_in_ref[:, 0:width])
    d_normed = d_normed + dot_cols(d_right.astype(BF16), point_in_ref[:, width : 2 * width])
    own_normed = normed_in[RIM : RIM + own]
    back = norm_back(d_normed * gain_in_ref[...], own_normed, inv_in[RIM : RIM + own])
    grad_ref[...] = (cot_ref[...].astype(F32) + back).astype(BF16)


def conv_module(place, lengths, parts, cotangents, gain_in, point_in, taps, gain_mid, point_out):
    own, width = cotangents[1].shape
    inner = own + RIM
    shape = jax.ShapeDtypeStruct((own, width), BF16)
    return pl.pallas_call(
        module_kernel,
        out_shape=(shape, shape),
        in_specs=[SMEM, SMEM] + [VMEM] * 12 + [HBM, VMEM, VMEM, HBM],
        out_specs=(VMEM, VMEM),
        scratch_shapes=[
            pltpu.VMEM((8, own + 2 * RIM, width), F32),
            pltpu.VMEM((8, own + 2 * RIM, 128), jnp.int32),
            pltpu.VMEM((inner, width), F32),
            pltpu.VMEM((own, width), F32),
            pltpu.VMEM(point_in.shape, BF16),
            pltpu.VMEM(point_out.shape, BF16),
            pltpu.SemaphoreType.DMA((2,)),
        ],
        compiler_params=pltpu.CompilerParams(vmem_limit_bytes=48 * 1024 * 1024),
        name="conv_module",
    )(place, lengths, *parts, *cotangents, gain_in[None], point_in, taps, gain_mid[None], point_out)
def send(place, frames, block_dest, proj_weight):
    blocks, width = frames.shape
    rows, columns = proj_weight.shape
    shape = jax.ShapeDtypeStruct((rows, columns // 2), BF16)
    return pl.pallas_call(
        send_kernel,
        out_shape=(jax.ShapeDtypeStruct((blocks, 2, width), BF16), shape, shape),
        in_specs=[SMEM, VMEM, VMEM, VMEM],
        out_specs=(VMEM, VMEM, VMEM),
        name="send",
    )(place, frames, block_dest, proj_weight)


def landing_slots(place, block_dest, groups, blocks):
    return pl.pallas_call(
        landing_kernel,
        out_shape=jax.ShapeDtypeStruct((2, groups, blocks), BF16),
        in_specs=[SMEM, VMEM],
        out_specs=VMEM,
        name="landing",
    )(place, block_dest)


def cut_matrix(seats, width):
    mel_bins = width // BLK
    share, frame, mel = np.meshgrid(
        np.arange(seats), np.arange(BLK), np.arange(PITCH), indexing="ij"
    )
    source = MEL_STEP * share - MEL_LEAD + mel
    fits = (mel < MEL_KEEP) & (source >= 0) & (source < mel_bins)
    source = np.where(fits, frame * mel_bins + source, -1).reshape(-1)
    return jnp.asarray(np.arange(width)[:, None] == source[None, :], BF16)


def place_blocks(place, arrived, landing, cotangent, seats):
    blocks = landing.shape[2]
    rim_rows = 16 * cotangent.shape[1] // WIDE
    rows = [blocks + (rim_rows if step in (1, seats - 1) else 0) for step in range(seats)]
    return pl.pallas_call(
        place_kernel,
        out_shape=[jax.ShapeDtypeStruct((count, WIDE), BF16) for count in rows],
        in_specs=[SMEM, VMEM, VMEM, VMEM, VMEM],
        out_specs=[VMEM] * seats,
        scratch_shapes=[pltpu.VMEM((blocks, seats * WIDE), BF16)],
        name="place",
    )(place, arrived, landing, cut_matrix(seats, arrived.shape[2]), cotangent)


def share_routes(groups, seats, flip):
    cluster = groups // seats
    routes = []
    for group in range(groups):
        for seat in range(seats):
            target = ((group // cluster) ^ seat) * cluster + (group % cluster ^ flip)
            routes.append((group * seats + seat, target * seats + seat))
    return routes


def gather_share(pair, groups, cluster):
    members = [
        [begin + core + 2 * index for index in range(cluster // 2)]
        for begin in range(0, groups, cluster)
        for core in range(2)
    ]
    rows, half = pair.shape
    copies = jnp.broadcast_to(pair[None], (cluster // 2, rows, half))
    same = lax.all_to_all(
        copies, "dp", split_axis=0, concat_axis=0, tiled=True, axis_index_groups=members
    ).reshape(-1, half)
    return same


def local(
    loader_frames,
    block_dest,
    utt_lengths,
    conv1_weight,
    conv2_weight,
    proj_weight,
    gain_in,
    point_in,
    taps,
    gain_mid,
    point_out,
    grad_encoded,
):
    groups, seats = lax.axis_size("dp"), lax.axis_size("seq")
    group, seat = lax.axis_index("dp"), lax.axis_index("seq")
    place = jnp.stack([group, seat]).astype(jnp.int32)
    lengths = utt_lengths[0]
    frames = loader_frames[0]
    blocks = frames.shape[0]
    cotangent = grad_encoded[0]
    own, width = cotangent.shape
    channels = conv2_weight.shape[1]
    rows = proj_weight.shape[0]
    cluster = groups // seats
    half = width // 2
    core = group % 2
    outgoing, same, other = send(place, frames, block_dest, proj_weight)
    same = lax.ppermute(same, ("dp", "seq"), share_routes(groups, seats, 0))
    other = lax.ppermute(other, ("dp", "seq"), share_routes(groups, seats, 1))
    arrived = lax.all_to_all(outgoing, "dp", split_axis=0, concat_axis=0, tiled=True)
    landing = landing_slots(place, block_dest, groups, blocks)
    windows = place_blocks(place, arrived, landing, cotangent, seats)
    pair = jnp.where(
        core == 0,
        jnp.concatenate([same, other], axis=0),
        jnp.concatenate([other, same], axis=0),
    )

    def ring(step):
        return [(index, (index + step) % seats) for index in range(seats)]

    windows = [windows[0]] + [
        lax.ppermute(windows[step], "seq", ring(step)) for step in range(1, seats)
    ]
    pair, *windows = lax.optimization_barrier((pair, *windows))
    same = gather_share(pair, groups, cluster)
    conv1 = jnp.pad(conv1_weight, ((0, 16 - conv1_weight.shape[0]), (0, 0)))
    features = conv_features(place, lengths, windows, conv1, conv2_weight, seats * own)
    features, same = lax.optimization_barrier((features, same))
    other = lax.ppermute(same, "dp", [(index, index ^ 1) for index in range(groups)])
    parts = []
    for proj in (same, other):
        sums = projected_parts(place, features, proj, seats)
        parts += [sums[0]] + [
            lax.ppermute(sums[step], "seq", ring(step)) for step in range(1, seats)
        ]
    encoded, grad_input = conv_module(
        place,
        lengths,
        parts,
        (windows[1], cotangent, windows[3]),
        gain_in,
        point_in,
        taps,
        gain_mid,
        point_out,
    )
    return encoded[None], grad_input[None]


def solution(mesh):
    placed = (
        P("seq", "dp", None),
        P("seq", None),
        P("dp", None),
        P(),
        P(),
        P("dp", None),
        P(),
        P(),
        P(),
        P(),
        P(),
        P("dp", "seq", None),
    )
    return jax.shard_map(
        local,
        mesh=mesh,
        in_specs=placed,
        out_specs=(P("dp", "seq", None), P("dp", "seq", None)),
        check_vma=False,
    )
```

```python
import functools

import jax
import jax.numpy as jnp
import numpy as np
from jax import lax
from jax.experimental import pallas as pl
from jax.experimental.pallas import tpu as pltpu
from jax.sharding import PartitionSpec as P

BLK = 8
PITCH = 32
WIDE = BLK * PITCH
MEL_STEP = 20
MEL_LEAD = 4
MEL_KEEP = 27
FULL = 4
BINS = FULL + 1
BINS_IN = 13
BIN_ORDER = tuple(range(0, BINS_IN, 2)) + tuple(range(1, BINS_IN, 2))
EVENS = (BINS_IN + 1) // 2
RIM = 32
PROJ_PARTS = 4
CONV_ROWS = 256
F32 = jnp.float32
BF16 = jnp.bfloat16
VMEM = pl.BlockSpec(memory_space=pltpu.VMEM)
SMEM = pl.BlockSpec(memory_space=pltpu.SMEM)
HBM = pl.BlockSpec(memory_space=pltpu.HBM)


def iota(shape, dim):
    return lax.broadcasted_iota(jnp.int32, shape, dim)


def one_hot(condition):
    return jnp.where(condition, 1.0, 0.0).astype(BF16)


def dot(left, right):
    return jnp.dot(left, right, preferred_element_type=F32)


def dot_rows(left, right):
    return lax.dot_general(left, right, (((0,), (0,)), ((), ())), preferred_element_type=F32)


def dot_cols(left, right):
    return lax.dot_general(left, right, (((1,), (1,)), ((), ())), preferred_element_type=F32)


def send_kernel(place_ref, frames_ref, dest_ref, proj_ref, out_ref, same_ref, other_ref):
    group = place_ref[0]
    blocks = frames_ref.shape[0]
    span = pl.multiple_of((group // 2) * 128, 128)
    pair = dest_ref[:, pl.ds(span, 128)]
    pair = jnp.where(group % 2 == 1, pltpu.roll(pair, 128 - blocks, 1), pair)
    row = jnp.broadcast_to(pair, (128, 128)) // blocks
    at_row, at_col = iota((128, 128), 0), iota((128, 128), 1)
    column = jnp.sum(jnp.where(at_row == at_col, row, 0), axis=1, keepdims=True)
    same = (row == column) & (at_row < at_col) & (at_row < blocks)
    rank = jnp.sum(jnp.where(same, 1, 0), axis=0, keepdims=True)
    slot = (row[0:1] * 2 + rank)[:, 0:blocks]
    sorted_blocks = dot(one_hot(iota((2 * blocks, blocks), 0) == slot), frames_ref[...])
    out_ref[...] = sorted_blocks.astype(BF16).reshape(out_ref.shape)
    half = same_ref.shape[1]
    left, right = proj_ref[:, 0:half], proj_ref[:, half : 2 * half]
    odd = group % 2 == 1
    same_ref[...] = jnp.where(odd, right, left)
    other_ref[...] = jnp.where(odd, left, right)


def landing_kernel(place_ref, dest_ref, out_ref):
    group = place_ref[0]
    _, groups, blocks = out_ref.shape
    rows = [dest_ref[:, at : at + 128] for at in range(0, groups * blocks, 128)]
    dest = jnp.concatenate(rows, axis=0)
    dest = jnp.concatenate([dest, pltpu.roll(dest, 128 - blocks, 1)], axis=0)[:, 0:blocks]
    at_row, at_col = iota((groups, groups), 0), iota((groups, groups), 1)
    pairs = groups // 2
    order = one_hot(at_row == jnp.where(at_col < pairs, 2 * at_col, 2 * (at_col - pairs) + 1))
    mine = dest // blocks == group
    earlier = one_hot(iota((blocks, blocks), 0) < iota((blocks, blocks), 1))
    rank = dot(one_hot(mine), earlier)
    spot = dest % blocks
    for copy in range(2):
        kept = jnp.where(mine & (rank == float(copy)), spot + 1, 0)
        landing = jnp.sum(kept, axis=1, keepdims=True) - 1
        landing = one_hot(iota((groups, blocks), 1) == landing)
        out_ref[copy] = dot(order, landing).astype(BF16)


def place_kernel(place_ref, arrived_ref, landing_ref, cut_ref, cot_ref, *out_refs):
    group, seat = place_ref[0], place_ref[1]
    window_ref = out_refs[-1]
    blocks = landing_ref.shape[2]
    arrived = arrived_ref[...]
    placed = dot_rows(landing_ref[0], arrived[:, 0, :]) + dot_rows(
        landing_ref[1], arrived[:, 1, :]
    )
    seats = len(out_refs) - 1
    window_ref[...] = dot(placed.astype(BF16), cut_ref[...]).astype(BF16)
    count = cot_ref.shape[0]
    for step in range(seats):
        share = ((seat + step) % seats) ^ (group // 16)
        span = pl.ds(pl.multiple_of(share * WIDE, WIDE), WIDE)
        out_refs[step][0:blocks, :] = window_ref[:, span]
        if step in (1, seats - 1):
            begin = count - 16 if step == 1 else 0
            for piece in range(cot_ref.shape[1] // WIDE):
                columns = slice(piece * WIDE, (piece + 1) * WIDE)
                rows = slice(blocks + 16 * piece, blocks + 16 * piece + 16)
                out_refs[step][rows, :] = cot_ref[begin : begin + 16, columns]


def row_starts(share):
    start_a = jnp.where(share == 0, 2176, jnp.where(share == 2, 128, 0))
    start_b = jnp.where(share == 1, 2304, jnp.where(share == 3, 256, 2432))
    return 128 * share + 128, start_a, start_b


def proj_copy(proj_hbm, proj_ref, sems, part):
    size = proj_hbm.shape[0] // PROJ_PARTS
    return pltpu.make_async_copy(
        proj_hbm.at[pl.ds(part * size, size)],
        proj_ref.at[pl.ds(128 + part * size, size)],
        sems.at[part],
    )


def project(features, share, proj_ref, wait):
    start, start_a, start_b = row_starts(share)
    result = None
    wait(0)
    for index in range(FULL + 2):
        if index < PROJ_PARTS - 1:
            wait(index + 1)
        if index < FULL:
            at, size, column = start + 512 * index, 512, 512 * index
        else:
            at, size = (start_a, 256) if index == FULL else (start_b, 256)
            column = 512 * FULL + 256 * (index - FULL)
        weight = proj_ref[pl.ds(pl.multiple_of(at, 128), size), :]
        part = dot(features(column, size), weight)
        result = part if result is None else result + part
    return result


def zero_rims(proj_ref, rows):
    rim = jnp.zeros((128, proj_ref.shape[1]), BF16)
    proj_ref[0:128, :] = rim
    proj_ref[128 + rows : 256 + rows, :] = rim


def conv_kernel(place_ref, lengths_ref, *refs):
    block_refs, (conv1_ref, conv2_hbm), refs = refs[:4], refs[4:6], refs[6:]
    out_ref, conv2_ref, patch_ref, first_ref, conv2_sems = refs
    group, seat = place_ref[0], place_ref[1]
    share = seat ^ (group // 16)
    taps, channels = conv2_ref.shape[0], conv2_ref.shape[1]
    frames = out_ref.shape[0]
    conv2_copies = [
        pltpu.make_async_copy(conv2_hbm.at[tap], conv2_ref.at[tap], conv2_sems.at[tap])
        for tap in range(taps)
    ]
    for copy in conv2_copies:
        copy.start()
    windows = jnp.concatenate([block_ref[0:64, :] for block_ref in block_refs], axis=0)
    count = windows.shape[0]
    frame = (seat * 128 + iota((frames, count), 0)) % (2 * count)
    block = iota((frames, count), 1)
    block = ((seat + 4 - block // 64) % 4) * 64 + block % 64
    own_block = frame // 2
    second = lengths_ref[0]
    third = second + lengths_ref[1]
    begins = (own_block == 0) | (own_block == second) | (own_block == third)
    odd = frame % 2 == 1
    here = own_block == block
    before = (own_block - 1 == block) & jnp.logical_not(begins)
    here_odd = dot(one_hot(odd & here), windows)
    here_even = dot(one_hot(jnp.logical_not(odd) & here), windows)
    prev_even = dot(one_hot(jnp.logical_not(odd) & before), windows)
    lane = iota((frames, WIDE), 1)
    patches = pltpu.roll(here_odd, WIDE - PITCH, 1) + pltpu.roll(
        jnp.where(lane < 5 * PITCH, here_even, prev_even), 3 * PITCH, 1
    )
    for index, mel_bin in enumerate(BIN_ORDER):
        moved = patches if mel_bin == 0 else pltpu.roll(patches, WIDE - 2 * mel_bin, 1)
        patch_ref[index * frames : (index + 1) * frames, :] = moved.astype(BF16)
    tap_lane, tap_at = iota((WIDE, 16), 0), iota((WIDE, 16), 1)
    all_rows = BINS_IN * frames
    for row_tap in range(3):
        spread = (2 * row_tap + tap_at // 3) * PITCH + tap_at % 3
        weight = dot(one_hot((tap_lane == spread) & (tap_at < 9)), conv1_ref[...]).astype(BF16)
        for start in range(0, all_rows, 512):
            stop = min(start + 512, all_rows)
            response = dot(patch_ref[start:stop, :], weight)
            first_ref[row_tap, start:stop, :] = jnp.maximum(response, 0.0).astype(BF16)
    whole_rows = (1, EVENS + 1, 2)
    half_rows = (0, EVENS, 1)
    bin_a = jnp.where(share == 0, 5, 0)
    bin_b = jnp.where(share == 3, 0, 5)
    side_a = jnp.where((share == 1) | (share == 2), 1, 0)
    side_b = jnp.where((share == 0) | (share == 3), 1, 0)
    half = channels // 2
    for copy in conv2_copies:
        copy.wait()
    for begin in range(0, frames, CONV_ROWS):
        for part in range(FULL):
            total = None
            for tap in range(taps):
                at = (whole_rows[tap % 3] + part) * frames + begin
                product = dot(first_ref[tap // 3, at : at + CONV_ROWS, :], conv2_ref[tap])
                total = product if total is None else total + product
            columns = slice(part * channels, (part + 1) * channels)
            out_ref[begin : begin + CONV_ROWS, columns] = jnp.maximum(total, 0.0).astype(BF16)
        for index, (mel_bin, side) in enumerate(((bin_a, side_a), (bin_b, side_b))):
            columns = pl.ds(pl.multiple_of(side * half, 128), half)
            total = None
            for tap in range(taps):
                at = (half_rows[tap % 3] + mel_bin) * frames + begin
                rows = pl.ds(pl.multiple_of(at, 128), CONV_ROWS)
                product = dot(first_ref[tap // 3, rows, :], conv2_ref[tap, :, columns])
                total = product if total is None else total + product
            first = FULL * channels + index * half
            columns = slice(first, first + half)
            out_ref[begin : begin + CONV_ROWS, columns] = jnp.maximum(total, 0.0).astype(BF16)


def conv_features(place, lengths, blocks, conv1_weight, conv2_weight, frames):
    taps, channels, _ = conv2_weight.shape
    return pl.pallas_call(
        conv_kernel,
        out_shape=jax.ShapeDtypeStruct((frames, BINS * channels), BF16),
        in_specs=[SMEM] * 2 + [VMEM] * 5 + [HBM],
        out_specs=VMEM,
        scratch_shapes=[
            pltpu.VMEM(conv2_weight.shape, BF16),
            pltpu.VMEM((BINS_IN * frames, WIDE), BF16),
            pltpu.VMEM((3, BINS_IN * frames, channels), BF16),
            pltpu.SemaphoreType.DMA((taps,)),
        ],
        compiler_params=pltpu.CompilerParams(vmem_limit_bytes=48 * 1024 * 1024),
        name="convolutions",
    )(place, lengths, *blocks, conv1_weight, conv2_weight)


def proj_kernel(place_ref, features_ref, proj_hbm, *refs):
    earlier_refs, refs = refs[:-7], refs[-7:]
    out_refs, (result_ref, proj_ref, sems) = refs[:4], refs[4:]
    half = proj_ref.shape[1]
    group, seat = place_ref[0], place_ref[1]
    for part in range(PROJ_PARTS):
        proj_copy(proj_hbm, proj_ref, sems, part).start()
    zero_rims(proj_ref, proj_hbm.shape[0])

    def features(column, size):
        return features_ref[:, column : column + size]

    def wait(part):
        proj_copy(proj_hbm, proj_ref, sems, part).wait()

    result = project(features, seat ^ (group // 16), proj_ref, wait)
    result_ref[...] = result.astype(BF16)
    count = result_ref.shape[0]
    own = count // len(out_refs)
    for step, out_ref in enumerate(out_refs):
        for at in range(0, own + 2 * RIM, RIM):
            source = (step * own - RIM + at) % count
            columns = slice(out_ref.shape[1] - half, out_ref.shape[1])
            out_ref[at : at + RIM, columns] = result_ref[source : source + RIM, :]
    for step, earlier_ref in zip((1, 3), earlier_refs):
        out_refs[step][:, 0:half] = earlier_ref[...]


def projected_parts(place, features, proj, seats, earlier=()):
    rows, half = proj.shape
    frames = features.shape[0]
    count = frames // seats + 2 * RIM
    widths = [2 * half if earlier and step in (1, 3) else half for step in range(seats)]
    return pl.pallas_call(
        proj_kernel,
        out_shape=[jax.ShapeDtypeStruct((count, width), BF16) for width in widths],
        in_specs=[SMEM, VMEM, HBM] + [VMEM] * len(earlier),
        out_specs=[VMEM] * seats,
        scratch_shapes=[
            pltpu.VMEM((frames, half), BF16),
            pltpu.VMEM((rows + 256, half), BF16),
            pltpu.SemaphoreType.DMA((PROJ_PARTS,)),
        ],
        compiler_params=pltpu.CompilerParams(vmem_limit_bytes=40 * 1024 * 1024),
        name="projection",
    )(place, features, proj, *earlier)


def layer_norm(values):
    average = jnp.mean(values, axis=-1, keepdims=True)
    centered = values - average
    inverse = lax.rsqrt(jnp.mean(centered * centered, axis=-1, keepdims=True) + 1e-05)
    return centered * inverse, inverse


def norm_back(d_normed, normed, inverse):
    return (
        d_normed
        - jnp.mean(d_normed, axis=-1, keepdims=True)
        - normed * jnp.mean(d_normed * normed, axis=-1, keepdims=True)
    ) * inverse


def depthwise(source, seg_ref, taps_ref, moved_ref, out_ref, base, seg_base, count, reverse):
    kernel, width = taps_ref.shape
    half = (kernel - 1) // 2
    length = source.shape[0]
    for residue in range(8):
        for index in range(width // 128):
            lanes = slice(index * 128, (index + 1) * 128)
            column = source[:, lanes]
            if residue:
                column = pltpu.roll(column, length - residue, 0)
            moved_ref[residue, 0:length, lanes] = column
    step = 32
    for begin in range(0, count, step):
        mine = seg_ref[0, seg_base + begin : seg_base + begin + step, :]
        running = [jnp.zeros((step, 128), F32) for _ in range(width // 128)]
        for offset in range(kernel):
            shift = half - offset if reverse else offset - half
            residue = shift % 8
            other = seg_base + begin + shift - residue
            same = seg_ref[residue, other : other + step, :] == mine
            at = base + begin + shift - residue
            for index in range(width // 128):
                lanes = slice(index * 128, (index + 1) * 128)
                window = jnp.where(same, moved_ref[residue, at : at + step, lanes], 0.0)
                running[index] = running[index] + window * taps_ref[offset : offset + 1, lanes]
        for index in range(width // 128):
            out_ref[begin : begin + step, index * 128 : (index + 1) * 128] = running[index]


def module_kernel(
    place_ref,
    lengths_ref,
    same_0_ref,
    same_2_ref,
    other_0_ref,
    other_2_ref,
    both_1_ref,
    both_3_ref,
    cot_low_ref,
    cot_ref,
    cot_high_ref,
    gain_in_ref,
    point_in_ref,
    taps_ref,
    gain_mid_ref,
    point_out_ref,
    encoded_ref,
    grad_ref,
    glu_ref,
    seg_ref,
    mixed_ref,
    back_ref,
):
    own, width = cot_ref.shape
    total = own + 2 * RIM
    inner = own + RIM
    skip = RIM // 2
    both = both_1_ref[...].astype(F32) + both_3_ref[...].astype(F32)
    side = width // 2
    same = same_0_ref[...].astype(F32) + same_2_ref[...].astype(F32) + both[:, 0:side]
    other = other_0_ref[...].astype(F32) + other_2_ref[...].astype(F32) + both[:, side:width]
    odd = place_ref[0] % 2 == 1
    halves = [jnp.where(odd, other, same), jnp.where(odd, same, other)]
    encoder = jnp.concatenate(halves, axis=1).astype(BF16).astype(F32)
    normed_in, inv_in = layer_norm(encoder)
    ln_in = (normed_in * gain_in_ref[...]).astype(BF16)
    left = dot(ln_in, point_in_ref[:, 0:width])
    gate = jax.nn.sigmoid(dot(ln_in, point_in_ref[:, width : 2 * width]))
    glu_out = (left * gate).astype(BF16).astype(F32)
    frame = place_ref[1] * own - RIM + iota((total, 128), 0)
    block = (frame + 4 * RIM) // 2 - 2 * RIM
    second = lengths_ref[0]
    third = second + lengths_ref[1]
    ends = third + lengths_ref[2]
    seg = (
        jnp.where(block >= 0, 1, 0)
        + jnp.where(block >= second, 1, 0)
        + jnp.where(block >= third, 1, 0)
        + jnp.where(block >= ends, 1, 0)
    )
    for residue in range(8):
        seg_ref[residue] = pltpu.roll(seg, total - residue, 0) if residue else seg
    depthwise(glu_out, seg_ref, taps_ref, glu_ref, mixed_ref, skip, skip, inner, False)
    normed_mid, inv_mid = layer_norm(mixed_ref[...])
    scaled = normed_mid * gain_mid_ref[...]
    logistic = jax.nn.sigmoid(scaled)
    slope = logistic * (1.0 + scaled * (1.0 - logistic))
    low = RIM - skip
    hidden = (scaled * logistic)[low : low + own].astype(BF16)
    encoded = encoder[RIM : RIM + own] + dot(hidden, point_out_ref[...])
    encoded_ref[...] = encoded.astype(BF16)
    low_edge, high_edge = [
        jnp.concatenate([ref[64 + 16 * piece : 80 + 16 * piece, :] for piece in range(3)], axis=1)
        for ref in (cot_low_ref, cot_high_ref)
    ]
    cotangent = jnp.concatenate([low_edge, cot_ref[...], high_edge], axis=0)
    d_hidden = dot_cols(cotangent, point_out_ref[...])
    d_mixed = norm_back(d_hidden * slope * gain_mid_ref[...], normed_mid, inv_mid)
    d_mixed = d_mixed.astype(BF16).astype(F32)
    depthwise(d_mixed, seg_ref, taps_ref, glu_ref, back_ref, low, RIM, own, True)
    d_glu = back_ref[...]
    own_gate = gate[RIM : RIM + own]
    d_left = d_glu * own_gate
    d_right = d_left * left[RIM : RIM + own] * (1.0 - own_gate)
    d_normed = dot_cols(d_left.astype(BF16), point_in_ref[:, 0:width])
    d_normed = d_normed + dot_cols(d_right.astype(BF16), point_in_ref[:, width : 2 * width])
    own_normed = normed_in[RIM : RIM + own]
    back = norm_back(d_normed * gain_in_ref[...], own_normed, inv_in[RIM : RIM + own])
    grad_ref[...] = (cot_ref[...].astype(F32) + back).astype(BF16)


def conv_module(place, lengths, parts, cotangents, gain_in, point_in, taps, gain_mid, point_out):
    own, width = cotangents[1].shape
    inner = own + RIM
    shape = jax.ShapeDtypeStruct((own, width), BF16)
    return pl.pallas_call(
        module_kernel,
        out_shape=(shape, shape),
        in_specs=[SMEM, SMEM] + [VMEM] * 14,
        out_specs=(VMEM, VMEM),
        scratch_shapes=[
            pltpu.VMEM((8, own + 2 * RIM, width), F32),
            pltpu.VMEM((8, own + 2 * RIM, 128), jnp.int32),
            pltpu.VMEM((inner, width), F32),
            pltpu.VMEM((own, width), F32),
        ],
        compiler_params=pltpu.CompilerParams(vmem_limit_bytes=48 * 1024 * 1024),
        name="conv_module",
    )(place, lengths, *parts, *cotangents, gain_in[None], point_in, taps, gain_mid[None], point_out)
def send(place, frames, block_dest, proj_weight):
    blocks, width = frames.shape
    rows, columns = proj_weight.shape
    shape = jax.ShapeDtypeStruct((rows, columns // 2), BF16)
    return pl.pallas_call(
        send_kernel,
        out_shape=(jax.ShapeDtypeStruct((blocks, 2, width), BF16), shape, shape),
        in_specs=[SMEM, VMEM, VMEM, VMEM],
        out_specs=(VMEM, VMEM, VMEM),
        name="send",
    )(place, frames, block_dest, proj_weight)


def landing_slots(place, block_dest, groups, blocks):
    return pl.pallas_call(
        landing_kernel,
        out_shape=jax.ShapeDtypeStruct((2, groups, blocks), BF16),
        in_specs=[SMEM, VMEM],
        out_specs=VMEM,
        name="landing",
    )(place, block_dest)


def cut_matrix(seats, width):
    mel_bins = width // BLK
    share, frame, mel = np.meshgrid(
        np.arange(seats), np.arange(BLK), np.arange(PITCH), indexing="ij"
    )
    source = MEL_STEP * share - MEL_LEAD + mel
    fits = (mel < MEL_KEEP) & (source >= 0) & (source < mel_bins)
    source = np.where(fits, frame * mel_bins + source, -1).reshape(-1)
    return jnp.asarray(np.arange(width)[:, None] == source[None, :], BF16)


def place_blocks(place, arrived, landing, cotangent, seats):
    blocks = landing.shape[2]
    rim_rows = 16 * cotangent.shape[1] // WIDE
    rows = [blocks + (rim_rows if step in (1, seats - 1) else 0) for step in range(seats)]
    return pl.pallas_call(
        place_kernel,
        out_shape=[jax.ShapeDtypeStruct((count, WIDE), BF16) for count in rows],
        in_specs=[SMEM, VMEM, VMEM, VMEM, VMEM],
        out_specs=[VMEM] * seats,
        scratch_shapes=[pltpu.VMEM((blocks, seats * WIDE), BF16)],
        name="place",
    )(place, arrived, landing, cut_matrix(seats, arrived.shape[2]), cotangent)


def share_routes(groups, seats, flip):
    cluster = groups // seats
    routes = []
    for group in range(groups):
        for seat in range(seats):
            target = ((group // cluster) ^ seat) * cluster + (group % cluster ^ flip)
            routes.append((group * seats + seat, target * seats + seat))
    return routes


def gather_share(pair, groups, cluster):
    members = [
        [begin + core + 2 * index for index in range(cluster // 2)]
        for begin in range(0, groups, cluster)
        for core in range(2)
    ]
    rows, half = pair.shape
    copies = jnp.broadcast_to(pair[None], (cluster // 2, rows, half))
    same = lax.all_to_all(
        copies, "dp", split_axis=0, concat_axis=0, tiled=True, axis_index_groups=members
    ).reshape(-1, half)
    return same


def local(
    loader_frames,
    block_dest,
    utt_lengths,
    conv1_weight,
    conv2_weight,
    proj_weight,
    gain_in,
    point_in,
    taps,
    gain_mid,
    point_out,
    grad_encoded,
):
    groups, seats = lax.axis_size("dp"), lax.axis_size("seq")
    group, seat = lax.axis_index("dp"), lax.axis_index("seq")
    place = jnp.stack([group, seat]).astype(jnp.int32)
    lengths = utt_lengths[0]
    frames = loader_frames[0]
    blocks = frames.shape[0]
    cotangent = grad_encoded[0]
    own, width = cotangent.shape
    channels = conv2_weight.shape[1]
    rows = proj_weight.shape[0]
    cluster = groups // seats
    half = width // 2
    core = group % 2
    outgoing, same, other = send(place, frames, block_dest, proj_weight)
    same = lax.ppermute(same, ("dp", "seq"), share_routes(groups, seats, 0))
    other = lax.ppermute(other, ("dp", "seq"), share_routes(groups, seats, 1))
    arrived = lax.all_to_all(outgoing, "dp", split_axis=0, concat_axis=0, tiled=True)
    landing = landing_slots(place, block_dest, groups, blocks)
    windows = place_blocks(place, arrived, landing, cotangent, seats)
    pair = jnp.where(
        core == 0,
        jnp.concatenate([same, other], axis=0),
        jnp.concatenate([other, same], axis=0),
    )

    def ring(step):
        return [(index, (index + step) % seats) for index in range(seats)]

    windows = [windows[0]] + [
        lax.ppermute(windows[step], "seq", ring(step)) for step in range(1, seats)
    ]
    pair, *windows = lax.optimization_barrier((pair, *windows))
    same = gather_share(pair, groups, cluster)
    conv1 = jnp.pad(conv1_weight, ((0, 16 - conv1_weight.shape[0]), (0, 0)))
    features = conv_features(place, lengths, windows, conv1, conv2_weight, seats * own)
    features, same = lax.optimization_barrier((features, same))
    other = lax.ppermute(same, "dp", [(index, index ^ 1) for index in range(groups)])
    first = projected_parts(place, features, same, seats)
    first_two = lax.ppermute(first[2], "seq", ring(2))
    second = projected_parts(place, features, other, seats, (first[1], first[3]))
    parts = [first[0], first_two, second[0]] + [
        lax.ppermute(second[step], "seq", ring(step)) for step in (2, 1, 3)
    ]
    encoded, grad_input = conv_module(
        place,
        lengths,
        parts,
        (windows[1], cotangent, windows[3]),
        gain_in,
        point_in,
        taps,
        gain_mid,
        point_out,
    )
    return encoded[None], grad_input[None]


def solution(mesh):
    placed = (
        P("seq", "dp", None),
        P("seq", None),
        P("dp", None),
        P(),
        P(),
        P("dp", None),
        P(),
        P(),
        P(),
        P(),
        P(),
        P("dp", "seq", None),
    )
    return jax.shard_map(
        local,
        mesh=mesh,
        in_specs=placed,
        out_specs=(P("dp", "seq", None), P("dp", "seq", None)),
        check_vma=False,
    )
```
